32 devices in a mesh: grp: 4 (over x, core), ep: 8 (over z, y).
Axes of the slice: x: 2, y: 2, z: 4, core: 2. Of those that a mesh axis runs over, the one named last changes fastest.
Arguments:
- tokens_in: bfloat16 [4096, 2048], P(('grp', 'ep')), may hold values from -6 to 6
- grad_out: bfloat16 [4096, 2048], P(('grp', 'ep')), may hold values from -6 to 6
- replica_of: int32 [4096, 2], P(('grp', 'ep')), may hold values from 0 to 31, all different within a row; in each aligned block of 128 rows (0 to 127, 128 to 255, ...) at most 16 rows name the same one
- gate_weights: bfloat16 [4096, 2], P(('grp', 'ep')), may hold values from 0.099609375 to 1
- placement: int32 [4, 8], replicated, may hold values from 0 to 1, as said below
- w_in_rep: bfloat16 [4, 8, 2048, 1024], P('grp', 'ep'), as said below
- w_down_rep: bfloat16 [4, 8, 2048, 512], P('grp', 'ep'), as said below
Outputs:
- d_tokens: bfloat16 [4096, 2048], P(('grp', 'ep'))
- d_gates: bfloat16 [4096, 2], P(('grp', 'ep'))
- grad_in: bfloat16 [16, 2048, 1024], P('ep', 'grp')
- grad_down: bfloat16 [16, 2048, 512], P('ep', 'grp')
The draws below stay inside these ranges and needn't reach their ends.
Inputs may be any that keep to these rules, and one draw needn't show every extreme that they name: `replica_of`: A row names a replica device by its index in the order grp then ep. The 2 rows of a token name different devices. At most 16 of the rows of one device name the same replica device, and some device sends exactly 16 rows to one replica. placement[g, e] selects expert e * 2 + placement[g, e]; in every column e each of the 2 values occurs at least once, so every expert has at least one copy. w_in_rep[g, e] and w_in_rep[g2, e] are equal wherever placement[g, e] equals placement[g2, e]. w_down_rep[g, e] and w_down_rep[g2, e] are equal wherever placement[g, e] equals placement[g2, e].
All inputs are finite; a program needn't handle non-finite values.
Results may differ from the reference program's by a relative error of at most 0.01.
Values may be sent and summed in bfloat16 or wider, within the bound.
A program may use at most 128 MiB of HBM per device.

```python
import math
import jax
import jax.numpy as jnp
import numpy as np
from jax import lax

D = 2048
H = 512
KPC = 2
TOP = 2
TOK_DEV = 128
EXPERTS = 16
TOKENS = 4096
CAP = 16
N_GRP = 4
N_EP = 8


def placement_plan(key):
    keys = jax.random.split(key, N_EP + 1)
    counts = jax.random.randint(keys[0], (N_EP,), 1, N_GRP)
    orders = jax.vmap(lambda single: jax.random.permutation(single, N_GRP))(keys[1:])
    plan = (orders >= counts[:, None]).astype(jnp.int32)
    return plan.T


def copies_of(key, canon):
    plan = placement_plan(jax.random.fold_in(key, 11))
    expert = jnp.arange(N_EP, dtype=jnp.int32)[None, :] * KPC + plan
    return canon[expert]


def draw_placement(key, part):
    return placement_plan(jax.random.fold_in(key, 11))


def draw_w_in_rep(key, part):
    inner = jax.random.fold_in(key, 23)
    canon = jax.random.normal(inner, (EXPERTS, D, 2 * H), jnp.float32) * D ** (-0.5)
    return copies_of(key, canon.astype(jnp.bfloat16))


def draw_w_down_rep(key, part):
    inner = jax.random.fold_in(key, 37)
    canon = jax.random.normal(inner, (EXPERTS, D, H), jnp.float32) * H ** (-0.5)
    return copies_of(key, canon.astype(jnp.bfloat16))


def levels(rng, shape, shards, smallest, largest):
    factor_of, own = 1.0, jax.random.fold_in(rng, 6)
    for axis_at, blocks in shards:
        heights = jnp.exp(jax.random.uniform(jax.random.fold_in(own, axis_at), (blocks,), jnp.float32, smallest / len(shards), largest / len(shards)))
        factor_of = factor_of * jnp.repeat(heights, shape[axis_at] // blocks).reshape([-1 if axis == axis_at else 1 for axis in range(len(shape))])
    return factor_of


def assign_block(key, own, number, rows, number_of, top, reach, skew):
    ranking = jax.random.permutation(key, number_of)
    packed, common = shares(number_of, rows * top, reach, skew, True), shares(number_of, rows * top, reach, skew, False)
    places = jnp.arange(number_of)

    def named(lengths, turn):
        used = int((lengths > 0).sum())
        fixed = max(1, used // 4)
        passed = fixed + (places - fixed + turn * (used - fixed)) % max(1, number_of - fixed)
        return jnp.zeros((number_of,), jnp.int32).at[ranking[jnp.where(places < fixed, places, passed)]].set(jnp.asarray(lengths, jnp.int32))

    lengths = jnp.where(number % 4 == 0, named(packed, number // 4), named(common, number - number // 4 - 1))
    mixed = jax.random.permutation(jax.random.fold_in(own, 3), number_of)
    giver, taker = mixed[0:number_of // 2 * 2:2], mixed[1:number_of // 2 * 2:2]
    margin = jnp.minimum(lengths[giver] - 1, reach - lengths[taker]) // 2
    margin = jnp.where((giver == ranking[0]) | (taker == ranking[0]) | (lengths[taker] == 0), 0, jnp.maximum(margin, 0))
    passed = jax.random.randint(jax.random.fold_in(own, 4), (number_of // 2,), 0, 1 << 20) % (margin + 1)
    lengths = lengths.at[giver].add(-passed).at[taker].add(passed)
    labels = jnp.searchsorted(jnp.cumsum(lengths), jnp.arange(rows * top), side="right").astype(jnp.int32)
    listing = labels.reshape(top, rows).T
    listing = listing[jax.random.permutation(jax.random.fold_in(own, 1), rows)]
    turn = jax.random.randint(jax.random.fold_in(own, 2), (rows, 1), 0, top)
    return jnp.take_along_axis(listing, (jnp.arange(top)[None, :] + turn) % top, axis=1)


def shares(amount, total, bound, lean, full):
    portions = [(1 << 20) // math.isqrt(standing ** lean) + 1 for standing in range(1, amount + 1)]
    largest = bound if full else min(bound, max(-(-total // amount), total * portions[0] // sum(portions)))
    least = 1 if total - largest >= amount - 1 else 0
    holding, surplus = [largest] + [least] * (amount - 1), total - largest - least * (amount - 1)
    while surplus > 0:
        movable = [i for i in range(1, amount) if holding[i] < largest] or [i for i in range(1, amount) if holding[i] < bound]
        mass, remaining = sum([portions[i] for i in movable]), surplus
        for i in movable:
            more = min(bound - holding[i], max(1, remaining * portions[i] // mass), surplus)
            holding[i] = holding[i] + more
            surplus = surplus - more
    return np.array(holding)


def bell_draw(key, shape, width, most, cuts=(), kind=jnp.bfloat16):
    gain = levels(key, shape, cuts, -0.22, 0.18) if cuts else 1.0
    array = jax.random.normal(key, shape, jnp.float32) * width * gain
    return jnp.minimum(jnp.maximum(array, -most), most).astype(kind)


def setup_inputs(seed: int = 0) -> dict:
    key_of = jax.random.split(jax.random.key(seed), 8)
    tokens_in = bell_draw(key_of[0], (TOKENS, D), 1.0, 6.0, ((0, 32),))
    grad_out = bell_draw(key_of[1], (TOKENS, D), 1.0, 6.0, ((0, 32),))
    replica_of_keys = jax.random.split(jax.random.fold_in(key_of[2], 1), TOKENS // TOK_DEV)
    replica_of_turns = jax.random.permutation(jax.random.fold_in(key_of[2], 3), TOKENS // TOK_DEV)
    replica_of = jax.vmap(lambda own, number: assign_block(jax.random.fold_in(key_of[2], 2), own, number, TOK_DEV, N_GRP * N_EP, TOP, CAP, 2))(replica_of_keys, replica_of_turns).reshape((TOKENS, TOP))
    gate_weights = jnp.clip(0.099609375 + 0.9003906 * jax.random.uniform(key_of[3], (TOKENS, TOP), jnp.float32) ** levels(key_of[3], (TOKENS, TOP), ((0, 32),), -0.2, 0.2), 0.099609375, 1.0).astype(jnp.bfloat16)
    placement = draw_placement(jax.random.fold_in(key_of[7], 71), 0)
    w_in_rep = draw_w_in_rep(jax.random.fold_in(key_of[7], 71), 0)
    w_down_rep = draw_w_down_rep(jax.random.fold_in(key_of[7], 71), 0)
    return {"tokens_in": tokens_in, "grad_out": grad_out, "replica_of": replica_of, "gate_weights": gate_weights, "placement": placement, "w_in_rep": w_in_rep, "w_down_rep": w_down_rep}


def expert_backward(rows_x, rows_dy, rows_gate, w_in, w_down):
    hidden = w_down.shape[1]
    both = jnp.dot(rows_x, w_in, preferred_element_type=jnp.float32)
    gate_pre = both[:, :hidden]
    up_part = both[:, hidden:]
    sigmoid_gate = jax.nn.sigmoid(gate_pre)
    silu_gate = gate_pre * sigmoid_gate
    activation = (silu_gate * up_part).astype(jnp.bfloat16)
    out_rows = lax.dot_general(activation, w_down, (((1,), (1,)), ((), ())), preferred_element_type=jnp.float32)
    gate_grad = jnp.sum(rows_dy.astype(jnp.float32) * out_rows, axis=1).astype(jnp.bfloat16)
    out_grad = (rows_gate.astype(jnp.float32)[:, None] * rows_dy.astype(jnp.float32)).astype(jnp.bfloat16)
    act_grad = jnp.dot(out_grad, w_down, preferred_element_type=jnp.float32)
    gate_grad_pre = act_grad * up_part * sigmoid_gate * (1.0 + gate_pre * (1.0 - sigmoid_gate))
    up_grad = act_grad * silu_gate
    both_grad = jnp.concatenate([gate_grad_pre, up_grad], axis=1).astype(jnp.bfloat16)
    row_grad = lax.dot_general(both_grad, w_in, (((1,), (1,)), ((), ())), preferred_element_type=jnp.float32).astype(jnp.bfloat16)
    part_in = lax.dot_general(rows_x, both_grad, (((0,), (0,)), ((), ())), preferred_element_type=jnp.float32)
    part_down = lax.dot_general(out_grad, activation, (((0,), (0,)), ((), ())), preferred_element_type=jnp.float32)
    return row_grad, gate_grad, part_in, part_down


def reference(tokens_in, grad_out, replica_of, gate_weights, placement, w_in_rep, w_down_rep):
    devices = N_GRP * N_EP
    per_device = TOK_DEV * TOP
    dest_rows = replica_of.reshape(devices, per_device)
    order_ids = jnp.arange(per_device, dtype=jnp.int32)

    def ranks(row_dest):
        earlier = (row_dest[:, None] == row_dest[None, :]) & (order_ids[None, :] < order_ids[:, None])
        return jnp.sum(earlier.astype(jnp.int32), axis=1).astype(jnp.int32)

    rank_in = lax.map(ranks, dest_rows)
    sources = jnp.arange(devices, dtype=jnp.int32)[:, None]
    global_slot = (dest_rows * (devices * CAP) + sources * CAP + rank_in).reshape(-1).astype(jnp.int32)
    row_ids = jnp.arange(devices * per_device, dtype=jnp.int32)
    slot_table = jnp.full((devices * devices * CAP,), -1, jnp.int32).at[global_slot].set(row_ids)
    flat_gate = gate_weights.reshape(-1)

    def step(carry, replica):
        acc_in, acc_down = carry
        start = (replica * devices * CAP).astype(jnp.int32)
        ids = lax.dynamic_slice(slot_table, (start,), (devices * CAP,))
        is_live = ids >= 0
        safe_ids = jnp.maximum(ids, 0)
        token_ids = safe_ids // TOP
        rows_x = jnp.where(is_live[:, None], tokens_in[token_ids], jnp.zeros((), tokens_in.dtype))
        rows_dy = jnp.where(is_live[:, None], grad_out[token_ids], jnp.zeros((), grad_out.dtype))
        rows_gate = jnp.where(is_live, flat_gate[safe_ids], jnp.zeros((), gate_weights.dtype))
        group = replica // N_EP
        column = replica % N_EP
        expert = column * KPC + placement[group, column]
        row_grad, gate_grad, part_in, part_down = expert_backward(rows_x, rows_dy, rows_gate, w_in_rep[group, column], w_down_rep[group, column])
        part_in = lax.optimization_barrier(part_in.astype(jnp.bfloat16)).astype(jnp.float32)
        part_down = lax.optimization_barrier(part_down.astype(jnp.bfloat16)).astype(jnp.float32)
        acc_in = acc_in.at[expert].add(part_in)
        acc_down = acc_down.at[expert].add(part_down)
        return (acc_in, acc_down), (row_grad, gate_grad)

    init = (jnp.zeros((EXPERTS, D, 2 * H), jnp.float32), jnp.zeros((EXPERTS, D, H), jnp.float32))
    (acc_in, acc_down), (all_rows, all_gates) = lax.scan(step, init, jnp.arange(devices, dtype=jnp.int32))
    row_grads = all_rows.reshape(-1, D)[global_slot]
    d_tokens = jnp.sum(row_grads.reshape(TOKENS, TOP, D).astype(jnp.float32), axis=1).astype(jnp.bfloat16)
    d_gates = all_gates.reshape(-1)[global_slot].reshape(TOKENS, TOP)
    return d_tokens, d_gates, acc_in.astype(jnp.bfloat16), acc_down.astype(jnp.bfloat16)
```

```python
import functools

import jax
import jax.numpy as jnp
from jax import lax
from jax.experimental import pallas as pl
from jax.experimental.pallas import tpu as pltpu
from jax.sharding import PartitionSpec as P

KPC = 2
MESH = pl.DeviceIdType.MESH
F32 = jnp.float32
BF16 = jnp.bfloat16
PIECES = 4


def dispatch_kernel(groups, lanes, inner, cap, tok_ref, rows_ref, held, picked,
                    up_send, down_send, chain_recv, plane_send, plane_recv, own_sem):
    tok_count, width = tok_ref.shape
    outer = lanes // inner
    plane = groups * inner
    my_group = lax.axis_index("grp")
    my_lane = lax.axis_index("ep")
    layer = my_lane // inner
    within = lax.rem(my_lane, inner)
    my_seat = my_group * inner + within
    step_rows = tok_count // PIECES

    def seat_id(seat):
        return (seat // inner, layer * inner + lax.rem(seat, inner))

    barrier = pltpu.get_barrier_semaphore()

    @pl.loop(1, plane)
    def _(off):
        pl.semaphore_signal(barrier, inc=1, device_id=seat_id(lax.rem(my_seat + off, plane)),
                            device_id_type=MESH)

    @pl.when(layer > 0)
    def _():
        pl.semaphore_signal(barrier, inc=1, device_id=(my_group, my_lane - inner),
                            device_id_type=MESH)

    @pl.when(layer < outer - 1)
    def _():
        pl.semaphore_signal(barrier, inc=1, device_id=(my_group, my_lane + inner),
                            device_id_type=MESH)

    ends = (layer > 0).astype(jnp.int32) + (layer < outer - 1).astype(jnp.int32)
    pl.semaphore_wait(barrier, plane - 1 + ends)

    def piece(source, part):
        return held.at[source, pl.ds(part * step_rows, step_rows)]

    def hop(source, part, upward, own):
        src = tok_ref.at[pl.ds(part * step_rows, step_rows)] if own else piece(source, part)
        sems = up_send if upward else down_send
        return pltpu.make_async_remote_copy(
            src_ref=src,
            dst_ref=piece(source, part),
            send_sem=sems.at[source, part],
            recv_sem=chain_recv.at[source, part],
            device_id=(my_group, my_lane + inner if upward else my_lane - inner),
            device_id_type=MESH,
        )

    def start_hops(source, part, own, come_up, come_down):
        if come_up:
            @pl.when(layer < outer - 1)
            def _():
                hop(source, part, True, own).start()
        if come_down:
            @pl.when(layer > 0)
            def _():
                hop(source, part, False, own).start()

    def spread(source, off):
        seat = lax.rem(my_seat + off, plane)
        return pltpu.make_async_remote_copy(
            src_ref=picked.at[source, seat],
            dst_ref=rows_ref.at[source, my_seat],
            send_sem=plane_send.at[source, off],
            recv_sem=plane_recv.at[source, off],
            device_id=seat_id(seat),
            device_id_type=MESH,
        )

    def own_copy(source):
        return pltpu.make_async_copy(
            picked.at[source, my_seat], rows_ref.at[source, my_seat], own_sem.at[source]
        )

    def pick(source, view):
        facts = view[:, width - 128:].astype(F32).T
        slots = lax.broadcasted_iota(jnp.int32, (plane * cap, tok_count), 0).astype(F32)
        here = layer.astype(F32)
        first = ((facts[2:3] == here) & (facts[4:5] == slots)).astype(F32)
        second = ((facts[3:4] == here) & (facts[5:6] == slots)).astype(F32)
        chosen = (first + second).astype(BF16)
        step = 1024
        for begin in range(0, width - 128, step):
            got = jnp.dot(chosen, view[:, begin:begin + step], preferred_element_type=F32)
            picked[source, :, :, begin:begin + step] = got.astype(BF16).reshape(plane, cap, step)
        weights = jnp.sum(first * facts[0:1] + second * facts[1:2], axis=1, keepdims=True)
        tail = jnp.broadcast_to(weights, (plane * cap, 128)).astype(BF16)
        picked[source, :, :, width - 128:] = tail.reshape(plane, cap, 128)
        own_copy(source).start()

        @pl.loop(1, plane)
        def _(off):
            spread(source, off).start()

    for part in range(PIECES):
        start_hops(layer, part, True, True, True)
    pick(layer, tok_ref)
    for far in range(1, outer):
        below = layer - far
        above = layer + far
        for part in range(PIECES):
            @pl.when(below >= 0)
            def _():
                hop(below, part, True, False).wait_recv()
                start_hops(below, part, False, True, False)

            @pl.when(above < outer)
            def _():
                hop(above, part, False, False).wait_recv()
                start_hops(above, part, False, False, True)

        @pl.when(below >= 0)
        def _():
            pick(below, held.at[below])

        @pl.when(above < outer)
        def _():
            pick(above, held.at[above])

    for source in range(outer):
        own_copy(source).wait()

        @pl.loop(1, plane)
        def _(off):
            spread(source, off).wait_recv()
            spread(source, off).wait_send()

        for part in range(PIECES):
            @pl.when((source <= layer) & (layer < outer - 1))
            def _():
                hop(source, part, True, False).wait_send()

            @pl.when((source >= layer) & (layer > 0))
            def _():
                hop(source, part, False, False).wait_send()


def return_kernel(groups, lanes, inner, cap, slots_ref, rows_ref, in_ref, down_ref,
                  tokens_ref, gates_ref, got_in, got_down,
                  back, row_send, row_recv, in_send, in_recv, down_send, down_recv, own_sem):
    tok_count = slots_ref.shape[0]
    width = rows_ref.shape[-1]
    devices = groups * lanes
    my_group = lax.axis_index("grp")
    my_lane = lax.axis_index("ep")
    me = my_group * lanes + my_lane

    barrier = pltpu.get_barrier_semaphore()

    @pl.loop(1, devices)
    def _(off):
        peer = lax.rem(me + off, devices)
        pl.semaphore_signal(barrier, inc=1, device_id=(peer // lanes, lax.rem(peer, lanes)),
                            device_id_type=MESH)

    pl.semaphore_wait(barrier, devices - 1)

    def row_copy(off):
        peer = lax.rem(me + off, devices)
        group = peer // lanes
        lane = lax.rem(peer, lanes)
        return pltpu.make_async_remote_copy(
            src_ref=rows_ref.at[lane // inner, group * inner + lax.rem(lane, inner)],
            dst_ref=back.at[me],
            send_sem=row_send.at[off],
            recv_sem=row_recv.at[off],
            device_id=(group, lane),
            device_id_type=MESH,
        )

    def sum_copy(src, dst, send, recv, off):
        group = lax.rem(my_group + off, groups)
        return pltpu.make_async_remote_copy(
            src_ref=src.at[group],
            dst_ref=dst.at[my_group],
            send_sem=send.at[off],
            recv_sem=recv.at[off],
            device_id=(group, my_lane),
            device_id_type=MESH,
        )

    own = [
        pltpu.make_async_copy(
            rows_ref.at[my_lane // inner, my_group * inner + lax.rem(my_lane, inner)],
            back.at[me], own_sem.at[0]),
        pltpu.make_async_copy(in_ref.at[my_group], got_in.at[my_group], own_sem.at[1]),
        pltpu.make_async_copy(down_ref.at[my_group], got_down.at[my_group], own_sem.at[2]),
    ]

    @pl.loop(1, devices)
    def _(off):
        row_copy(off).start()

    for off in range(1, groups):
        sum_copy(in_ref, got_in, in_send, in_recv, off).start()
        sum_copy(down_ref, got_down, down_send, down_recv, off).start()
    for copy in own:
        copy.start()

    own[0].wait()

    @pl.loop(1, devices)
    def _(off):
        row_copy(off).wait_recv()

    places = lax.broadcasted_iota(jnp.int32, (tok_count, devices * cap), 1)
    first = (slots_ref[:, 0:1] == places).astype(F32)
    second = (slots_ref[:, 1:2] == places).astype(F32)
    both = (first + second).astype(BF16)
    step = 512
    for begin in range(0, width - 128, step):
        view = back[:, :, begin:begin + step].reshape(devices * cap, step)
        tokens_ref[:, begin:begin + step] = jnp.dot(
            both, view, preferred_element_type=F32).astype(BF16)
    tail = back[:, :, width - 128:].reshape(devices * cap, 128)
    gate_first = jnp.dot(first.astype(BF16), tail, preferred_element_type=F32)
    gate_second = jnp.dot(second.astype(BF16), tail, preferred_element_type=F32)
    lane_ids = lax.broadcasted_iota(jnp.int32, (tok_count, 128), 1)
    gates_ref[...] = jnp.where(lane_ids == 0, gate_first, gate_second).astype(BF16)

    own[1].wait()
    own[2].wait()
    for off in range(1, groups):
        sum_copy(in_ref, got_in, in_send, in_recv, off).wait()
        sum_copy(down_ref, got_down, down_send, down_recv, off).wait()

    @pl.loop(1, devices)
    def _(off):
        row_copy(off).wait_send()


def expert_backward(rows_x, rows_dy, rows_gate, w_in, w_down):
    hidden = w_down.shape[1]
    both = jnp.dot(rows_x, w_in, preferred_element_type=jnp.float32)
    gate_pre = both[:, :hidden]
    up_part = both[:, hidden:]
    sigmoid_gate = jax.nn.sigmoid(gate_pre)
    silu_gate = gate_pre * sigmoid_gate
    activation = (silu_gate * up_part).astype(jnp.bfloat16)
    out_rows = lax.dot_general(
        activation, w_down, (((1,), (1,)), ((), ())), preferred_element_type=jnp.float32
    )
    gate_grad = jnp.sum(rows_dy.astype(jnp.float32) * out_rows, axis=1).astype(jnp.bfloat16)
    out_grad = (rows_gate.astype(jnp.float32)[:, None] * rows_dy.astype(jnp.float32)).astype(
        jnp.bfloat16
    )
    act_grad = jnp.dot(out_grad, w_down, preferred_element_type=jnp.float32)
    gate_grad_pre = act_grad * up_part * sigmoid_gate * (1.0 + gate_pre * (1.0 - sigmoid_gate))
    up_grad = act_grad * silu_gate
    both_grad = jnp.concatenate([gate_grad_pre, up_grad], axis=1).astype(jnp.bfloat16)
    row_grad = lax.dot_general(
        both_grad, w_in, (((1,), (1,)), ((), ())), preferred_element_type=jnp.float32
    ).astype(jnp.bfloat16)
    part_in = lax.dot_general(
        rows_x, both_grad, (((0,), (0,)), ((), ())), preferred_element_type=jnp.float32
    )
    part_down = lax.dot_general(
        out_grad, activation, (((0,), (0,)), ((), ())), preferred_element_type=jnp.float32
    )
    return (row_grad, gate_grad, part_in, part_down)


def plain_shards(tokens_in, grad_out, replica_of, gate_weights, placement, w_in_rep, w_down_rep):
    tok_count, model_width = tokens_in.shape
    top_count = replica_of.shape[1]
    group_count = lax.axis_size("grp")
    lane_count = lax.axis_size("ep")
    device_count = group_count * lane_count
    capacity = max(2, 2 * tok_count * top_count // device_count)
    w_in = w_in_rep[0, 0]
    w_down = w_down_rep[0, 0]
    dest_rows = replica_of.reshape(-1)
    row_count = tok_count * top_count
    row_ids = jnp.arange(row_count, dtype=jnp.int32)
    earlier = (dest_rows[:, None] == dest_rows[None, :]) & (row_ids[None, :] < row_ids[:, None])
    rank_in = jnp.sum(earlier.astype(jnp.int32), axis=1)
    send_slot = dest_rows * capacity + rank_in
    slot_table = jnp.full((device_count * capacity,), -1, jnp.int32).at[send_slot].set(row_ids)
    is_live = slot_table >= 0
    safe_ids = jnp.maximum(slot_table, 0)
    token_ids = safe_ids // top_count
    send_x = jnp.where(is_live[:, None], tokens_in[token_ids], jnp.zeros((), tokens_in.dtype))
    send_dy = jnp.where(is_live[:, None], grad_out[token_ids], jnp.zeros((), grad_out.dtype))
    send_gate = jnp.where(
        is_live, gate_weights.reshape(-1)[safe_ids], jnp.zeros((), gate_weights.dtype)
    )
    block_shape = (group_count, lane_count, capacity, model_width)
    outgoing = (
        send_x.reshape(block_shape),
        send_dy.reshape(block_shape),
        send_gate.reshape(group_count, lane_count, capacity),
    )
    arrived = (
        lax.all_to_all(
            lax.all_to_all(outgoing[0], "ep", split_axis=1, concat_axis=1, tiled=True),
            "grp",
            split_axis=0,
            concat_axis=0,
            tiled=True,
        ),
        lax.all_to_all(
            lax.all_to_all(outgoing[1], "ep", split_axis=1, concat_axis=1, tiled=True),
            "grp",
            split_axis=0,
            concat_axis=0,
            tiled=True,
        ),
        lax.all_to_all(
            lax.all_to_all(outgoing[2], "ep", split_axis=1, concat_axis=1, tiled=True),
            "grp",
            split_axis=0,
            concat_axis=0,
            tiled=True,
        ),
    )
    rows_x = arrived[0].reshape(device_count * capacity, model_width)
    rows_dy = arrived[1].reshape(device_count * capacity, model_width)
    rows_gate = arrived[2].reshape(device_count * capacity)
    row_grad, gate_grad, part_in, part_down = expert_backward(
        rows_x, rows_dy, rows_gate, w_in, w_down
    )
    returning = (
        row_grad.reshape(block_shape),
        gate_grad.reshape(group_count, lane_count, capacity),
    )
    came_back = (
        lax.all_to_all(
            lax.all_to_all(returning[0], "grp", split_axis=0, concat_axis=0, tiled=True),
            "ep",
            split_axis=1,
            concat_axis=1,
            tiled=True,
        ),
        lax.all_to_all(
            lax.all_to_all(returning[1], "grp", split_axis=0, concat_axis=0, tiled=True),
            "ep",
            split_axis=1,
            concat_axis=1,
            tiled=True,
        ),
    )
    grads_rows = came_back[0].reshape(device_count * capacity, model_width)[send_slot]
    d_tokens = jnp.sum(
        grads_rows.reshape(tok_count, top_count, model_width).astype(jnp.float32), axis=1
    ).astype(jnp.bfloat16)
    d_gates = came_back[1].reshape(-1)[send_slot].reshape(tok_count, top_count)
    group_index = lax.axis_index("grp")
    column_index = lax.axis_index("ep")
    my_slot = placement[group_index, column_index]
    slot_mask = (jnp.arange(KPC, dtype=jnp.int32) == my_slot).astype(jnp.float32)
    stack_in = slot_mask[:, None, None] * part_in[None]
    stack_down = slot_mask[:, None, None] * part_down[None]
    summed_in, summed_down = (
        lax.psum_scatter(
            stack_in.astype(jnp.bfloat16), "grp", scatter_dimension=1, tiled=True
        ).astype(jnp.float32),
        lax.psum_scatter(
            stack_down.astype(jnp.bfloat16), "grp", scatter_dimension=1, tiled=True
        ).astype(jnp.float32),
    )
    return (d_tokens, d_gates, summed_in.astype(jnp.bfloat16), summed_down.astype(jnp.bfloat16))


def shards(tokens_in, grad_out, replica_of, gate_weights, placement, w_in_rep, w_down_rep):
    tok_count, width = tokens_in.shape
    top_count = replica_of.shape[1]
    groups = lax.axis_size("grp")
    lanes = lax.axis_size("ep")
    devices = groups * lanes
    cap = max(2, 2 * tok_count * top_count // devices)
    if cap % 16 or top_count != 2:
        return plain_shards(
            tokens_in, grad_out, replica_of, gate_weights, placement, w_in_rep, w_down_rep
        )
    inner = max(1, min(lanes, tok_count // (groups * cap)))
    outer = lanes // inner
    plane = groups * inner
    w_in = w_in_rep[0, 0]
    w_down = w_down_rep[0, 0]
    hidden = w_down.shape[1]
    dest_rows = replica_of.reshape(-1)
    row_ids = jnp.arange(tok_count * top_count, dtype=jnp.int32)
    earlier = (dest_rows[:, None] == dest_rows[None, :]) & (row_ids[None, :] < row_ids[:, None])
    rank_in = jnp.sum(earlier.astype(jnp.int32), axis=1).reshape(tok_count, top_count)
    lane_of = replica_of % lanes
    seat_of = replica_of // lanes * inner + lane_of % inner
    facts = jnp.concatenate(
        [
            gate_weights,
            (lane_of // inner).astype(BF16),
            (seat_of * cap + rank_in).astype(BF16),
            jnp.zeros((tok_count, 128 - 3 * top_count), BF16),
        ],
        axis=1,
    )
    tok = jnp.concatenate([tokens_in, grad_out, facts], axis=1)
    full = tok.shape[1]
    any_spec = pl.BlockSpec(memory_space=pl.ANY)
    vmem_spec = pl.BlockSpec(memory_space=pltpu.VMEM)
    dma = pltpu.SemaphoreType.DMA
    rows = pl.pallas_call(
        functools.partial(dispatch_kernel, groups, lanes, inner, cap),
        out_shape=jax.ShapeDtypeStruct((outer, plane, cap, full), BF16),
        in_specs=[vmem_spec],
        out_specs=any_spec,
        scratch_shapes=[
            pltpu.VMEM((outer, tok_count, full), BF16),
            pltpu.VMEM((outer, plane, cap, full), BF16),
            dma((outer, PIECES)),
            dma((outer, PIECES)),
            dma((outer, PIECES)),
            dma((outer, plane)),
            dma((outer, plane)),
            dma((outer,)),
        ],
        compiler_params=pltpu.CompilerParams(
            collective_id=0, has_side_effects=True, vmem_limit_bytes=40 * 2**20
        ),
        name="dispatch",
    )(tok)
    row_total = devices * cap
    rows = rows.reshape(row_total, full)
    row_grad, gate_grad, part_in, part_down = expert_backward(
        rows[:, :width], rows[:, width:2 * width], rows[:, 2 * width], w_in, w_down
    )
    returned = jnp.concatenate(
        [row_grad, jnp.broadcast_to(gate_grad[:, None], (row_total, 128))], axis=1
    ).reshape(outer, plane, cap, width + 128)
    share = width // groups
    d_tokens, gates, got_in, got_down = pl.pallas_call(
        functools.partial(return_kernel, groups, lanes, inner, cap),
        out_shape=(
            jax.ShapeDtypeStruct((tok_count, width), BF16),
            jax.ShapeDtypeStruct((tok_count, 128), BF16),
            jax.ShapeDtypeStruct((groups, share, 2 * hidden), BF16),
            jax.ShapeDtypeStruct((groups, share, hidden), BF16),
        ),
        in_specs=[vmem_spec, any_spec, any_spec, any_spec],
        out_specs=(vmem_spec, vmem_spec, any_spec, any_spec),
        scratch_shapes=[
            pltpu.VMEM((devices, cap, width + 128), BF16),
            dma((devices,)),
            dma((devices,)),
            dma((groups,)),
            dma((groups,)),
            dma((groups,)),
            dma((groups,)),
            dma((3,)),
        ],
        compiler_params=pltpu.CompilerParams(
            collective_id=1, has_side_effects=True, vmem_limit_bytes=40 * 2**20
        ),
        name="give_back",
    )(
        replica_of * cap + rank_in,
        returned,
        part_in.astype(BF16).reshape(groups, share, 2 * hidden),
        part_down.astype(BF16).reshape(groups, share, hidden),
    )
    column = placement[:, lax.axis_index("ep")]
    mask = (column[None, :] == jnp.arange(KPC, dtype=jnp.int32)[:, None])[:, :, None, None]
    zero = jnp.zeros((), F32)
    summed_in = jnp.sum(jnp.where(mask, got_in[None].astype(F32), zero), axis=1)
    summed_down = jnp.sum(jnp.where(mask, got_down[None].astype(F32), zero), axis=1)
    return d_tokens, gates[:, :top_count], summed_in.astype(BF16), summed_down.astype(BF16)


def solution(mesh):
    placed = (
        P(("grp", "ep"), None),
        P(("grp", "ep"), None),
        P(("grp", "ep"), None),
        P(("grp", "ep"), None),
        P(),
        P("grp", "ep", None, None),
        P("grp", "ep", None, None),
    )
    return jax.shard_map(
        shards,
        mesh=mesh,
        in_specs=placed,
        out_specs=(
            P(("grp", "ep"), None),
            P(("grp", "ep"), None),
            P("ep", "grp", None),
            P("ep", "grp", None),
        ),
        check_vma=False,
    )
```

```python
import functools

import jax
import jax.numpy as jnp
from jax import lax
from jax.experimental import pallas as pl
from jax.experimental.pallas import tpu as pltpu
from jax.sharding import PartitionSpec as P

KPC = 2
MESH = pl.DeviceIdType.MESH
F32 = jnp.float32
BF16 = jnp.bfloat16
PIECES = 4


def layer_kernel(groups, lanes, inner, cap, tok_ref, slots_ref, mask_ref, w_in_hbm, w_down_hbm,
                 tokens_ref, gates_ref, grad_in_ref, grad_down_ref,
                 held, picked, rows, w_in, w_down, both_grads, gated, row_grads, back,
                 part_in, part_down, got_in, got_down,
                 up_send, down_send, chain_recv, plane_send, plane_recv, own_sem, load_sem,
                 row_send, row_recv, row_own, in_send, in_recv, down_sent, down_recv):
    tok_count, full = tok_ref.shape
    width = (full - 128) // 2
    hidden = w_down.shape[1]
    outer = lanes // inner
    plane = groups * inner
    devices = groups * lanes
    batch = plane * cap
    share = width // groups
    my_group = lax.axis_index("grp")
    my_lane = lax.axis_index("ep")
    me = my_group * lanes + my_lane
    layer = my_lane // inner
    my_seat = my_group * inner + lax.rem(my_lane, inner)
    step_rows = tok_count // PIECES

    load_in = pltpu.make_async_copy(w_in_hbm, w_in, load_sem.at[0])
    load_down = pltpu.make_async_copy(w_down_hbm, w_down, load_sem.at[1])
    load_in.start()
    load_down.start()

    barrier = pltpu.get_barrier_semaphore()

    @pl.loop(1, devices)
    def _(off):
        peer = lax.rem(me + off, devices)
        pl.semaphore_signal(barrier, inc=1, device_id=(peer // lanes, lax.rem(peer, lanes)),
                            device_id_type=MESH)

    pl.semaphore_wait(barrier, devices - 1)

    def piece(source, part):
        return held.at[source, pl.ds(part * step_rows, step_rows)]

    def hop(source, part, upward, own):
        src = tok_ref.at[pl.ds(part * step_rows, step_rows)] if own else piece(source, part)
        sems = up_send if upward else down_send
        return pltpu.make_async_remote_copy(
            src_ref=src,
            dst_ref=piece(source, part),
            send_sem=sems.at[source, part],
            recv_sem=chain_recv.at[source, part],
            device_id=(my_group, my_lane + inner if upward else my_lane - inner),
            device_id_type=MESH,
        )

    def spread(source, off):
        seat = lax.rem(my_seat + off, plane)
        return pltpu.make_async_remote_copy(
            src_ref=picked.at[source, seat],
            dst_ref=rows.at[source, my_seat],
            send_sem=plane_send.at[source, off],
            recv_sem=plane_recv.at[source, off],
            device_id=(seat // inner, layer * inner + lax.rem(seat, inner)),
            device_id_type=MESH,
        )

    def own_copy(source):
        return pltpu.make_async_copy(
            picked.at[source, my_seat], rows.at[source, my_seat], own_sem.at[source]
        )

    def row_copy(source, seat):
        return pltpu.make_async_remote_copy(
            src_ref=row_grads.at[source, seat],
            dst_ref=back.at[me],
            send_sem=row_send.at[source, seat],
            recv_sem=row_recv.at[me],
            device_id=(seat // inner, source * inner + lax.rem(seat, inner)),
            device_id_type=MESH,
        )

    def row_arrival(peer):
        return pltpu.make_async_remote_copy(
            src_ref=row_grads.at[0, 0],
            dst_ref=back.at[peer],
            send_sem=row_send.at[0, 0],
            recv_sem=row_recv.at[peer],
            device_id=(peer // lanes, lax.rem(peer, lanes)),
            device_id_type=MESH,
        )

    row_stay = pltpu.make_async_copy(row_grads.at[layer, my_seat], back.at[me], row_own)

    def sum_copies(group, slot):
        return [
            pltpu.make_async_remote_copy(
                src_ref=src.at[group],
                dst_ref=dst.at[my_group],
                send_sem=send.at[slot],
                recv_sem=recv.at[slot],
                device_id=(group, my_lane),
                device_id_type=MESH,
            )
            for src, dst, send, recv in (
                (part_in, got_in, in_send, in_recv),
                (part_down, got_down, down_sent, down_recv),
            )
        ]

    def pick(source, view):
        facts = view[:, full - 128:].astype(F32).T
        slots = lax.broadcasted_iota(jnp.int32, (batch, tok_count), 0).astype(F32)
        here = layer.astype(F32)
        first = ((facts[2:3] == here) & (facts[4:5] == slots)).astype(F32)
        second = ((facts[3:4] == here) & (facts[5:6] == slots)).astype(F32)
        chosen = (first + second).astype(BF16)
        step = 1024
        for begin in range(0, full - 128, step):
            got = jnp.dot(chosen, view[:, begin:begin + step], preferred_element_type=F32)
            picked[source, :, :, begin:begin + step] = got.astype(BF16).reshape(plane, cap, step)
        weights = jnp.sum(first * facts[0:1] + second * facts[1:2], axis=1, keepdims=True)
        tail = jnp.broadcast_to(weights, (batch, 128)).astype(BF16)
        picked[source, :, :, full - 128:] = tail.reshape(plane, cap, 128)
        own_copy(source).start()

        @pl.loop(1, plane)
        def _(off):
            spread(source, off).start()

    def work(source):
        own_copy(source).wait()

        @pl.loop(1, plane)
        def _(off):
            spread(source, off).wait_recv()

        row_x = rows[source, :, :, :width].reshape(batch, width)
        row_dy = rows[source, :, :, width:2 * width].reshape(batch, width)
        weight = rows[source, :, :, 2 * width:].reshape(batch, 128)[:, :1].astype(F32)
        both = jnp.dot(row_x, w_in[...], preferred_element_type=F32)
        back_act = jnp.dot(row_dy, w_down[...], preferred_element_type=F32)
        gate_pre = both[:, :hidden]
        up_part = both[:, hidden:]
        sig = jax.nn.sigmoid(gate_pre)
        silu = gate_pre * sig
        act = silu * up_part
        gate_grad = jnp.sum(act * back_act, axis=1, keepdims=True)
        act_grad = weight * back_act
        gated[source] = (weight * act).astype(BF16)
        gate_side = act_grad * up_part * sig * (1.0 + gate_pre * (1.0 - sig))
        both_grads[source, :, :hidden] = gate_side.astype(BF16)
        both_grads[source, :, hidden:] = (act_grad * silu).astype(BF16)
        step = 512
        for begin in range(0, width, step):
            got = lax.dot_general(
                both_grads[source], w_in[begin:begin + step, :], (((1,), (1,)), ((), ())),
                preferred_element_type=F32)
            row_grads[source, :, :, begin:begin + step] = got.astype(BF16).reshape(
                plane, cap, step)
        row_grads[source, :, :, width:] = jnp.broadcast_to(gate_grad, (batch, 128)).astype(
            BF16).reshape(plane, cap, 128)

        @pl.loop(0, plane)
        def _(seat):
            mine = (source == layer) & (seat == my_seat)

            @pl.when(mine)
            def _():
                row_stay.start()

            @pl.when(jnp.logical_not(mine))
            def _():
                row_copy(source, seat).start()

    below_count = layer
    above_count = outer - 1 - layer
    paired = jnp.minimum(below_count, above_count)

    def turn(q):
        odd = lax.rem(q, 2)
        in_pairs = (q <= 2 * paired).astype(jnp.int32)
        far = in_pairs * ((q + 1) // 2) + (1 - in_pairs) * (q - paired)
        longer = (below_count > above_count).astype(jnp.int32)
        from_below = in_pairs * odd + (1 - in_pairs) * longer
        return layer + far - 2 * far * from_below, from_below

    for part in range(PIECES):
        @pl.when(layer < outer - 1)
        def _():
            hop(layer, part, True, True).start()

        @pl.when(layer > 0)
        def _():
            hop(layer, part, False, True).start()
    pick(layer, tok_ref)
    load_in.wait()
    load_down.wait()

    @pl.loop(1, outer + 1)
    def _(q):
        @pl.when(q < outer)
        def _():
            source, from_below = turn(q)
            for part in range(PIECES):
                hop(source, part, True, False).wait_recv()

                @pl.when((from_below == 1) & (layer < outer - 1))
                def _():
                    hop(source, part, True, False).start()

                @pl.when((from_below == 0) & (layer > 0))
                def _():
                    hop(source, part, False, False).start()
            pick(source, held.at[source])

        work(turn(q - 1)[0])

    total = outer * batch
    grads = both_grads[...].reshape(total, 2 * hidden)
    acts = gated[...].reshape(total, hidden)

    @pl.loop(0, groups)
    def _(i):
        off = lax.rem(i + groups // 2, groups)
        group = lax.rem(my_group + off, groups)
        columns = pl.ds(pl.multiple_of(group * share, share), share)
        late = pl.ds(pl.multiple_of(width + group * share, share), share)
        some_x = rows[:, :, :, columns].reshape(total, share)
        part_in[group] = lax.dot_general(
            some_x, grads, (((0,), (0,)), ((), ())), preferred_element_type=F32).astype(BF16)
        some_dy = rows[:, :, :, late].reshape(total, share)
        part_down[group] = lax.dot_general(
            some_dy, acts, (((0,), (0,)), ((), ())), preferred_element_type=F32).astype(BF16)

        @pl.when(off > 0)
        def _():
            for copy in sum_copies(group, off):
                copy.start()

    row_stay.wait()

    @pl.loop(1, devices)
    def _(off):
        row_arrival(lax.rem(me + off, devices)).wait_recv()

    places = lax.broadcasted_iota(jnp.int32, (tok_count, devices * cap), 1)
    first = (slots_ref[:, 0:1] == places).astype(F32)
    second = (slots_ref[:, 1:2] == places).astype(F32)
    chosen = (first + second).astype(BF16)
    for begin in range(0, width, 512):
        view = back[:, :, begin:begin + 512].reshape(devices * cap, 512)
        tokens_ref[:, begin:begin + 512] = jnp.dot(
            chosen, view, preferred_element_type=F32).astype(BF16)
    tail = back[:, :, width:].reshape(devices * cap, 128)
    gate_first = jnp.dot(first.astype(BF16), tail, preferred_element_type=F32)
    gate_second = jnp.dot(second.astype(BF16), tail, preferred_element_type=F32)
    lane_ids = lax.broadcasted_iota(jnp.int32, (tok_count, 128), 1)
    gates_ref[...] = jnp.where(lane_ids == 0, gate_first, gate_second).astype(BF16)

    got_in[my_group] = part_in[my_group]
    got_down[my_group] = part_down[my_group]
    for off in range(1, groups):
        for copy in sum_copies(lax.rem(my_group + off, groups), off):
            copy.wait()

    @pl.loop(0, share // 16)
    def _(i):
        at = pl.ds(pl.multiple_of(i * 16, 16), 16)
        for got, out in ((got_in, grad_in_ref), (got_down, grad_down_ref)):
            blocks = [got[group, at].astype(F32) for group in range(groups)]
            for expert in range(KPC):
                flags = [mask_ref[expert * groups + group:expert * groups + group + 1, :1]
                         for group in range(groups)]
                out[expert, at] = sum(
                    flag * block for flag, block in zip(flags, blocks)).astype(BF16)

    for source in range(outer):
        @pl.loop(1, plane)
        def _(off):
            spread(source, off).wait_send()

        @pl.loop(0, plane)
        def _(seat):
            @pl.when(jnp.logical_not((source == layer) & (seat == my_seat)))
            def _():
                row_copy(source, seat).wait_send()

        for part in range(PIECES):
            @pl.when((source <= layer) & (layer < outer - 1))
            def _():
                hop(source, part, True, False).wait_send()

            @pl.when((source >= layer) & (layer > 0))
            def _():
                hop(source, part, False, False).wait_send()


def expert_backward(rows_x, rows_dy, rows_gate, w_in, w_down):
    hidden = w_down.shape[1]
    both = jnp.dot(rows_x, w_in, preferred_element_type=jnp.float32)
    gate_pre = both[:, :hidden]
    up_part = both[:, hidden:]
    sigmoid_gate = jax.nn.sigmoid(gate_pre)
    silu_gate = gate_pre * sigmoid_gate
    activation = (silu_gate * up_part).astype(jnp.bfloat16)
    out_rows = lax.dot_general(
        activation, w_down, (((1,), (1,)), ((), ())), preferred_element_type=jnp.float32
    )
    gate_grad = jnp.sum(rows_dy.astype(jnp.float32) * out_rows, axis=1).astype(jnp.bfloat16)
    out_grad = (rows_gate.astype(jnp.float32)[:, None] * rows_dy.astype(jnp.float32)).astype(
        jnp.bfloat16
    )
    act_grad = jnp.dot(out_grad, w_down, preferred_element_type=jnp.float32)
    gate_grad_pre = act_grad * up_part * sigmoid_gate * (1.0 + gate_pre * (1.0 - sigmoid_gate))
    up_grad = act_grad * silu_gate
    both_grad = jnp.concatenate([gate_grad_pre, up_grad], axis=1).astype(jnp.bfloat16)
    row_grad = lax.dot_general(
        both_grad, w_in, (((1,), (1,)), ((), ())), preferred_element_type=jnp.float32
    ).astype(jnp.bfloat16)
    part_in = lax.dot_general(
        rows_x, both_grad, (((0,), (0,)), ((), ())), preferred_element_type=jnp.float32
    )
    part_down = lax.dot_general(
        out_grad, activation, (((0,), (0,)), ((), ())), preferred_element_type=jnp.float32
    )
    return (row_grad, gate_grad, part_in, part_down)


def plain_shards(tokens_in, grad_out, replica_of, gate_weights, placement, w_in_rep, w_down_rep):
    tok_count, model_width = tokens_in.shape
    top_count = replica_of.shape[1]
    group_count = lax.axis_size("grp")
    lane_count = lax.axis_size("ep")
    device_count = group_count * lane_count
    capacity = max(2, 2 * tok_count * top_count // device_count)
    w_in = w_in_rep[0, 0]
    w_down = w_down_rep[0, 0]
    dest_rows = replica_of.reshape(-1)
    row_count = tok_count * top_count
    row_ids = jnp.arange(row_count, dtype=jnp.int32)
    earlier = (dest_rows[:, None] == dest_rows[None, :]) & (row_ids[None, :] < row_ids[:, None])
    rank_in = jnp.sum(earlier.astype(jnp.int32), axis=1)
    send_slot = dest_rows * capacity + rank_in
    slot_table = jnp.full((device_count * capacity,), -1, jnp.int32).at[send_slot].set(row_ids)
    is_live = slot_table >= 0
    safe_ids = jnp.maximum(slot_table, 0)
    token_ids = safe_ids // top_count
    send_x = jnp.where(is_live[:, None], tokens_in[token_ids], jnp.zeros((), tokens_in.dtype))
    send_dy = jnp.where(is_live[:, None], grad_out[token_ids], jnp.zeros((), grad_out.dtype))
    send_gate = jnp.where(
        is_live, gate_weights.reshape(-1)[safe_ids], jnp.zeros((), gate_weights.dtype)
    )
    block_shape = (group_count, lane_count, capacity, model_width)
    outgoing = (
        send_x.reshape(block_shape),
        send_dy.reshape(block_shape),
        send_gate.reshape(group_count, lane_count, capacity),
    )
    arrived = (
        lax.all_to_all(
            lax.all_to_all(outgoing[0], "ep", split_axis=1, concat_axis=1, tiled=True),
            "grp",
            split_axis=0,
            concat_axis=0,
            tiled=True,
        ),
        lax.all_to_all(
            lax.all_to_all(outgoing[1], "ep", split_axis=1, concat_axis=1, tiled=True),
            "grp",
            split_axis=0,
            concat_axis=0,
            tiled=True,
        ),
        lax.all_to_all(
            lax.all_to_all(outgoing[2], "ep", split_axis=1, concat_axis=1, tiled=True),
            "grp",
            split_axis=0,
            concat_axis=0,
            tiled=True,
        ),
    )
    rows_x = arrived[0].reshape(device_count * capacity, model_width)
    rows_dy = arrived[1].reshape(device_count * capacity, model_width)
    rows_gate = arrived[2].reshape(device_count * capacity)
    row_grad, gate_grad, part_in, part_down = expert_backward(
        rows_x, rows_dy, rows_gate, w_in, w_down
    )
    returning = (
        row_grad.reshape(block_shape),
        gate_grad.reshape(group_count, lane_count, capacity),
    )
    came_back = (
        lax.all_to_all(
            lax.all_to_all(returning[0], "grp", split_axis=0, concat_axis=0, tiled=True),
            "ep",
            split_axis=1,
            concat_axis=1,
            tiled=True,
        ),
        lax.all_to_all(
            lax.all_to_all(returning[1], "grp", split_axis=0, concat_axis=0, tiled=True),
            "ep",
            split_axis=1,
            concat_axis=1,
            tiled=True,
        ),
    )
    grads_rows = came_back[0].reshape(device_count * capacity, model_width)[send_slot]
    d_tokens = jnp.sum(
        grads_rows.reshape(tok_count, top_count, model_width).astype(jnp.float32), axis=1
    ).astype(jnp.bfloat16)
    d_gates = came_back[1].reshape(-1)[send_slot].reshape(tok_count, top_count)
    group_index = lax.axis_index("grp")
    column_index = lax.axis_index("ep")
    my_slot = placement[group_index, column_index]
    slot_mask = (jnp.arange(KPC, dtype=jnp.int32) == my_slot).astype(jnp.float32)
    stack_in = slot_mask[:, None, None] * part_in[None]
    stack_down = slot_mask[:, None, None] * part_down[None]
    summed_in, summed_down = (
        lax.psum_scatter(
            stack_in.astype(jnp.bfloat16), "grp", scatter_dimension=1, tiled=True
        ).astype(jnp.float32),
        lax.psum_scatter(
            stack_down.astype(jnp.bfloat16), "grp", scatter_dimension=1, tiled=True
        ).astype(jnp.float32),
    )
    return (d_tokens, d_gates, summed_in.astype(jnp.bfloat16), summed_down.astype(jnp.bfloat16))


def shards(tokens_in, grad_out, replica_of, gate_weights, placement, w_in_rep, w_down_rep):
    tok_count, width = tokens_in.shape
    top_count = replica_of.shape[1]
    groups = lax.axis_size("grp")
    lanes = lax.axis_size("ep")
    devices = groups * lanes
    cap = max(2, 2 * tok_count * top_count // devices)
    if cap % 16 or top_count != 2:
        return plain_shards(
            tokens_in, grad_out, replica_of, gate_weights, placement, w_in_rep, w_down_rep
        )
    inner = max(1, min(lanes, tok_count // (groups * cap)))
    outer = lanes // inner
    plane = groups * inner
    w_in = w_in_rep[0, 0]
    w_down = w_down_rep[0, 0]
    hidden = w_down.shape[1]
    dest_rows = replica_of.reshape(-1)
    row_ids = jnp.arange(tok_count * top_count, dtype=jnp.int32)
    earlier = (dest_rows[:, None] == dest_rows[None, :]) & (row_ids[None, :] < row_ids[:, None])
    rank_in = jnp.sum(earlier.astype(jnp.int32), axis=1).reshape(tok_count, top_count)
    lane_of = replica_of % lanes
    seat_of = replica_of // lanes * inner + lane_of % inner
    facts = jnp.concatenate(
        [
            gate_weights,
            (lane_of // inner).astype(BF16),
            (seat_of * cap + rank_in).astype(BF16),
            jnp.zeros((tok_count, 128 - 3 * top_count), BF16),
        ],
        axis=1,
    )
    tok = jnp.concatenate([tokens_in, grad_out, facts], axis=1)
    full = tok.shape[1]
    any_spec = pl.BlockSpec(memory_space=pl.ANY)
    vmem_spec = pl.BlockSpec(memory_space=pltpu.VMEM)
    dma = pltpu.SemaphoreType.DMA
    share = width // groups
    column = placement[:, lax.axis_index("ep")]
    held_here = column[None, :] == jnp.arange(KPC, dtype=jnp.int32)[:, None]
    mask = jnp.broadcast_to(held_here.astype(F32).reshape(KPC * groups, 1), (KPC * groups, 128))
    batch = plane * cap
    d_tokens, gates, grad_in, grad_down = pl.pallas_call(
        functools.partial(layer_kernel, groups, lanes, inner, cap),
        out_shape=(
            jax.ShapeDtypeStruct((tok_count, width), BF16),
            jax.ShapeDtypeStruct((tok_count, 128), BF16),
            jax.ShapeDtypeStruct((KPC, share, 2 * hidden), BF16),
            jax.ShapeDtypeStruct((KPC, share, hidden), BF16),
        ),
        in_specs=[vmem_spec, vmem_spec, vmem_spec, any_spec, any_spec],
        out_specs=(vmem_spec,) * 4,
        scratch_shapes=[
            pltpu.VMEM((outer, tok_count, full), BF16),
            pltpu.VMEM((outer, plane, cap, full), BF16),
            pltpu.VMEM((outer, plane, cap, full), BF16),
            pltpu.VMEM((width, 2 * hidden), BF16),
            pltpu.VMEM((width, hidden), BF16),
            pltpu.VMEM((outer, batch, 2 * hidden), BF16),
            pltpu.VMEM((outer, batch, hidden), BF16),
            pltpu.VMEM((outer, plane, cap, width + 128), BF16),
            pltpu.VMEM((devices, cap, width + 128), BF16),
            pltpu.VMEM((groups, share, 2 * hidden), BF16),
            pltpu.VMEM((groups, share, hidden), BF16),
            pltpu.VMEM((groups, share, 2 * hidden), BF16),
            pltpu.VMEM((groups, share, hidden), BF16),
            dma((outer, PIECES)),
            dma((outer, PIECES)),
            dma((outer, PIECES)),
            dma((outer, plane)),
            dma((outer, plane)),
            dma((outer,)),
            dma((2,)),
            dma((outer, plane)),
            dma((devices,)),
            dma,
            dma((groups,)),
            dma((groups,)),
            dma((groups,)),
            dma((groups,)),
        ],
        compiler_params=pltpu.CompilerParams(
            collective_id=0, has_side_effects=True, vmem_limit_bytes=58 * 2**20
        ),
        name="layer_backward",
    )(tok, replica_of * cap + rank_in, mask, w_in, w_down)
    return d_tokens, gates[:, :top_count], grad_in, grad_down


def solution(mesh):
    placed = (
        P(("grp", "ep"), None),
        P(("grp", "ep"), None),
        P(("grp", "ep"), None),
        P(("grp", "ep"), None),
        P(),
        P("grp", "ep", None, None),
        P("grp", "ep", None, None),
    )
    return jax.shard_map(
        shards,
        mesh=mesh,
        in_specs=placed,
        out_specs=(
            P(("grp", "ep"), None),
            P(("grp", "ep"), None),
            P("ep", "grp", None),
            P("ep", "grp", None),
        ),
        check_vma=False,
    )
```

```python
import functools

import jax
import jax.numpy as jnp
from jax import lax
from jax.experimental import pallas as pl
from jax.experimental.pallas import tpu as pltpu
from jax.sharding import PartitionSpec as P

KPC = 2
MESH = pl.DeviceIdType.MESH
F32 = jnp.float32
BF16 = jnp.bfloat16
PIECES = 4


def layer_kernel(groups, lanes, inner, cap, tok_ref, slots_ref, mask_ref, w_in_hbm, w_down_hbm,
                 tokens_ref, gates_ref, grad_in_ref, grad_down_ref,
                 held, picked, rows, w_in, w_down, other_in, other_down,
                 both_grads, gated, row_grads, back,
                 sib_in, sib_down, from_in, from_down, cross_in, cross_down, got_in, got_down,
                 up_send, down_send, chain_recv, plane_send, plane_recv, own_sem, load_sem,
                 row_send, row_recv, row_own, swap_send, swap_recv, sib_send, sib_recv,
                 cross_send, cross_recv):
    tok_count, full = tok_ref.shape
    width = (full - 128) // 2
    hidden = w_down.shape[1]
    outer = lanes // inner
    plane = groups // 2 * inner
    devices = groups * lanes
    batch = plane * cap
    senders = groups // 2 * lanes
    share = width // groups
    my_group = lax.axis_index("grp")
    my_lane = lax.axis_index("ep")
    me = my_group * lanes + my_lane
    layer = my_lane // inner
    side = my_group // 2
    core = lax.rem(my_group, 2)
    my_seat = side * inner + lax.rem(my_lane, inner)
    my_sender = side * lanes + my_lane
    sibling = (side * 2 + 1 - core, my_lane)
    across = ((1 - side) * 2 + core, my_lane)
    step_rows = tok_count // PIECES

    load_in = pltpu.make_async_copy(w_in_hbm, w_in, load_sem.at[0])
    load_down = pltpu.make_async_copy(w_down_hbm, w_down, load_sem.at[1])
    load_in.start()
    load_down.start()

    barrier = pltpu.get_barrier_semaphore()

    @pl.loop(1, devices)
    def _(off):
        peer = lax.rem(me + off, devices)
        pl.semaphore_signal(barrier, inc=1, device_id=(peer // lanes, lax.rem(peer, lanes)),
                            device_id_type=MESH)

    pl.semaphore_wait(barrier, devices - 1)

    def remote(src, dst, send, recv, device):
        return pltpu.make_async_remote_copy(
            src_ref=src, dst_ref=dst, send_sem=send, recv_sem=recv,
            device_id=device, device_id_type=MESH)

    swaps = [
        remote(w_in_hbm, other_in, swap_send.at[0], swap_recv.at[0], sibling),
        remote(w_down_hbm, other_down, swap_send.at[1], swap_recv.at[1], sibling),
    ]
    for swap in swaps:
        swap.start()

    def piece(source, part):
        return held.at[source, pl.ds(part * step_rows, step_rows)]

    def hop(source, part, upward, own):
        src = tok_ref.at[pl.ds(part * step_rows, step_rows)] if own else piece(source, part)
        sems = up_send if upward else down_send
        return pltpu.make_async_remote_copy(
            src_ref=src,
            dst_ref=piece(source, part),
            send_sem=sems.at[source, part],
            recv_sem=chain_recv.at[source, part],
            device_id=(my_group, my_lane + inner if upward else my_lane - inner),
            device_id_type=MESH,
        )

    def spread(source, off):
        seat = lax.rem(my_seat + off, plane)
        return pltpu.make_async_remote_copy(
            src_ref=picked.at[source, seat],
            dst_ref=rows.at[source, my_seat],
            send_sem=plane_send.at[source, off],
            recv_sem=plane_recv.at[source, off],
            device_id=(seat // inner * 2 + core, layer * inner + lax.rem(seat, inner)),
            device_id_type=MESH,
        )

    def own_copy(source):
        return pltpu.make_async_copy(
            picked.at[source, my_seat], rows.at[source, my_seat], own_sem.at[source]
        )

    def row_copy(source, seat):
        return pltpu.make_async_remote_copy(
            src_ref=row_grads.at[source, seat],
            dst_ref=back.at[my_sender],
            send_sem=row_send.at[source, seat],
            recv_sem=row_recv.at[my_sender],
            device_id=(seat // inner * 2 + core, source * inner + lax.rem(seat, inner)),
            device_id_type=MESH,
        )

    def row_arrival(peer):
        return pltpu.make_async_remote_copy(
            src_ref=row_grads.at[0, 0],
            dst_ref=back.at[peer],
            send_sem=row_send.at[0, 0],
            recv_sem=row_recv.at[peer],
            device_id=(peer // lanes * 2 + core, lax.rem(peer, lanes)),
            device_id_type=MESH,
        )

    row_stay = pltpu.make_async_copy(row_grads.at[layer, my_seat], back.at[my_sender], row_own)

    def pick(source, view):
        facts = view[:, full - 128:].astype(F32).T
        slots = lax.broadcasted_iota(jnp.int32, (batch, tok_count), 0).astype(F32)
        here = layer.astype(F32)
        first = ((facts[2:3] == here) & (facts[4:5] == slots)).astype(F32)
        second = ((facts[3:4] == here) & (facts[5:6] == slots)).astype(F32)
        chosen = (first + second).astype(BF16)
        step = 1024
        for begin in range(0, full - 128, step):
            got = jnp.dot(chosen, view[:, begin:begin + step], preferred_element_type=F32)
            picked[source, :, :, begin:begin + step] = got.astype(BF16).reshape(plane, cap, step)
        weights = jnp.sum(first * facts[0:1] + second * facts[1:2], axis=1, keepdims=True)
        tail = jnp.broadcast_to(weights, (batch, 128)).astype(BF16)
        picked[source, :, :, full - 128:] = tail.reshape(plane, cap, 128)
        own_copy(source).start()

        @pl.loop(1, plane)
        def _(off):
            spread(source, off).start()

    def work(source):
        own_copy(source).wait()

        @pl.loop(1, plane)
        def _(off):
            spread(source, off).wait_recv()

        row_x = rows[source, :, :, :width].reshape(batch, width)
        row_dy = rows[source, :, :, width:2 * width].reshape(batch, width)
        weight = rows[source, :, :, 2 * width:].reshape(batch, 128)[:, :1].astype(F32)
        both = jnp.dot(row_x, w_in[...], preferred_element_type=F32)
        back_act = jnp.dot(row_dy, w_down[...], preferred_element_type=F32)
        gate_pre = both[:, :hidden]
        up_part = both[:, hidden:]
        sig = jax.nn.sigmoid(gate_pre)
        silu = gate_pre * sig
        act = silu * up_part
        gate_grad = jnp.sum(act * back_act, axis=1, keepdims=True)
        act_grad = weight * back_act
        gated[source] = (weight * act).astype(BF16)
        gate_side = act_grad * up_part * sig * (1.0 + gate_pre * (1.0 - sig))
        both_grads[source, :, :hidden] = gate_side.astype(BF16)
        both_grads[source, :, hidden:] = (act_grad * silu).astype(BF16)
        step = 512
        for begin in range(0, width, step):
            got = lax.dot_general(
                both_grads[source], w_in[begin:begin + step, :], (((1,), (1,)), ((), ())),
                preferred_element_type=F32)
            row_grads[source, :, :, begin:begin + step] = got.astype(BF16).reshape(
                plane, cap, step)
        row_grads[source, :, :, width:] = jnp.broadcast_to(gate_grad, (batch, 128)).astype(
            BF16).reshape(plane, cap, 128)

        @pl.loop(0, plane)
        def _(seat):
            mine = (source == layer) & (seat == my_seat)

            @pl.when(mine)
            def _():
                row_stay.start()

            @pl.when(jnp.logical_not(mine))
            def _():
                row_copy(source, seat).start()

    below_count = layer
    above_count = outer - 1 - layer
    paired = jnp.minimum(below_count, above_count)

    def turn(q):
        odd = lax.rem(q, 2)
        in_pairs = (q <= 2 * paired).astype(jnp.int32)
        far = in_pairs * ((q + 1) // 2) + (1 - in_pairs) * (q - paired)
        longer = (below_count > above_count).astype(jnp.int32)
        from_below = in_pairs * odd + (1 - in_pairs) * longer
        return layer + far - 2 * far * from_below, from_below

    for part in range(PIECES):
        @pl.when(layer < outer - 1)
        def _():
            hop(layer, part, True, True).start()

        @pl.when(layer > 0)
        def _():
            hop(layer, part, False, True).start()
    pick(layer, tok_ref)
    load_in.wait()
    load_down.wait()
    for swap in swaps:
        swap.wait()

    @pl.loop(0, width // 64)
    def _(i):
        at = pl.ds(pl.multiple_of(i * 64, 64), 64)
        mine = mask_ref[0:1, :1].astype(BF16)
        theirs = mask_ref[1:2, :1].astype(BF16)
        w_in[at] = mine * w_in[at] + theirs * other_in[at]
        w_down[at] = mine * w_down[at] + theirs * other_down[at]

    @pl.loop(1, outer + 1)
    def _(q):
        @pl.when(q < outer)
        def _():
            source, from_below = turn(q)
            for part in range(PIECES):
                hop(source, part, True, False).wait_recv()

                @pl.when((from_below == 1) & (layer < outer - 1))
                def _():
                    hop(source, part, True, False).start()

                @pl.when((from_below == 0) & (layer > 0))
                def _():
                    hop(source, part, False, False).start()
            pick(source, held.at[source])

        work(turn(q - 1)[0])

    total = outer * batch
    grads = both_grads[...].reshape(total, 2 * hidden)
    acts = gated[...].reshape(total, hidden)

    def part_of(group, begin, other):
        columns = pl.ds(pl.multiple_of(begin + group * share, share), share)
        some = rows[:, :, :, columns].reshape(total, share)
        return lax.dot_general(some, other, (((0,), (0,)), ((), ())), preferred_element_type=F32)

    kinds = (
        (0, grads, sib_in, from_in, cross_in, got_in, grad_in_ref),
        (width, acts, sib_down, from_down, cross_down, got_down, grad_down_ref),
    )

    def to_sibling(kind, which):
        return remote(kinds[kind][2].at[which], kinds[kind][3].at[which],
                      sib_send.at[kind, which], sib_recv.at[kind, which], sibling)

    def to_across(kind):
        return remote(kinds[kind][4], kinds[kind][5], cross_send.at[kind], cross_recv.at[kind],
                      across)

    for which, target in ((0, 1 - side), (1, side)):
        for kind in range(2):
            begin, other, sib = kinds[kind][:3]
            sib[which] = part_of(target * 2 + 1 - core, begin, other).astype(BF16)
            to_sibling(kind, which).start()
        for kind in range(2):
            begin, other, _, arrived, crossing, _, out = kinds[kind]
            mine = part_of(target * 2 + core, begin, other)
            to_sibling(kind, which).wait_recv()
            joined = (mine + arrived[which].astype(F32)).astype(BF16)
            if which == 0:
                crossing[...] = joined
                to_across(kind).start()
            else:
                out[0] = joined

    row_stay.wait()

    @pl.loop(1, senders)
    def _(off):
        row_arrival(lax.rem(my_sender + off, senders)).wait_recv()

    places = lax.broadcasted_iota(jnp.int32, (tok_count, senders * cap), 1)
    first = (slots_ref[:, 0:1] == places).astype(F32)
    second = (slots_ref[:, 1:2] == places).astype(F32)
    chosen = (first + second).astype(BF16)
    for begin in range(0, width, 512):
        view = back[:, :, begin:begin + 512].reshape(senders * cap, 512)
        tokens_ref[:, begin:begin + 512] = jnp.dot(
            chosen, view, preferred_element_type=F32).astype(BF16)
    tail = back[:, :, width:].reshape(senders * cap, 128)
    gate_first = jnp.dot(first.astype(BF16), tail, preferred_element_type=F32)
    gate_second = jnp.dot(second.astype(BF16), tail, preferred_element_type=F32)
    lane_ids = lax.broadcasted_iota(jnp.int32, (tok_count, 128), 1)
    gates_ref[...] = jnp.where(lane_ids == 0, gate_first, gate_second).astype(BF16)

    for kind in range(2):
        to_across(kind).wait()
        to_sibling(kind, 0).wait_send()
        to_sibling(kind, 1).wait_send()

    @pl.loop(0, share // 16)
    def _(i):
        at = pl.ds(pl.multiple_of(i * 16, 16), 16)
        for kind in range(2):
            got, out = kinds[kind][5:]
            near = out[0, at].astype(F32)
            away = got[at].astype(F32)
            lower = mask_ref[2:3, :1]
            upper = mask_ref[3:4, :1]
            out[0, at] = (lower * near + upper * away).astype(BF16)
            out[1, at] = (upper * near + lower * away).astype(BF16)

    for source in range(outer):
        @pl.loop(1, plane)
        def _(off):
            spread(source, off).wait_send()

        @pl.loop(0, plane)
        def _(seat):
            @pl.when(jnp.logical_not((source == layer) & (seat == my_seat)))
            def _():
                row_copy(source, seat).wait_send()

        for part in range(PIECES):
            @pl.when((source <= layer) & (layer < outer - 1))
            def _():
                hop(source, part, True, False).wait_send()

            @pl.when((source >= layer) & (layer > 0))
            def _():
                hop(source, part, False, False).wait_send()


def expert_backward(rows_x, rows_dy, rows_gate, w_in, w_down):
    hidden = w_down.shape[1]
    both = jnp.dot(rows_x, w_in, preferred_element_type=jnp.float32)
    gate_pre = both[:, :hidden]
    up_part = both[:, hidden:]
    sigmoid_gate = jax.nn.sigmoid(gate_pre)
    silu_gate = gate_pre * sigmoid_gate
    activation = (silu_gate * up_part).astype(jnp.bfloat16)
    out_rows = lax.dot_general(
        activation, w_down, (((1,), (1,)), ((), ())), preferred_element_type=jnp.float32
    )
    gate_grad = jnp.sum(rows_dy.astype(jnp.float32) * out_rows, axis=1).astype(jnp.bfloat16)
    out_grad = (rows_gate.astype(jnp.float32)[:, None] * rows_dy.astype(jnp.float32)).astype(
        jnp.bfloat16
    )
    act_grad = jnp.dot(out_grad, w_down, preferred_element_type=jnp.float32)
    gate_grad_pre = act_grad * up_part * sigmoid_gate * (1.0 + gate_pre * (1.0 - sigmoid_gate))
    up_grad = act_grad * silu_gate
    both_grad = jnp.concatenate([gate_grad_pre, up_grad], axis=1).astype(jnp.bfloat16)
    row_grad = lax.dot_general(
        both_grad, w_in, (((1,), (1,)), ((), ())), preferred_element_type=jnp.float32
    ).astype(jnp.bfloat16)
    part_in = lax.dot_general(
        rows_x, both_grad, (((0,), (0,)), ((), ())), preferred_element_type=jnp.float32
    )
    part_down = lax.dot_general(
        out_grad, activation, (((0,), (0,)), ((), ())), preferred_element_type=jnp.float32
    )
    return (row_grad, gate_grad, part_in, part_down)


def plain_shards(tokens_in, grad_out, replica_of, gate_weights, placement, w_in_rep, w_down_rep):
    tok_count, model_width = tokens_in.shape
    top_count = replica_of.shape[1]
    group_count = lax.axis_size("grp")
    lane_count = lax.axis_size("ep")
    device_count = group_count * lane_count
    capacity = max(2, 2 * tok_count * top_count // device_count)
    w_in = w_in_rep[0, 0]
    w_down = w_down_rep[0, 0]
    dest_rows = replica_of.reshape(-1)
    row_count = tok_count * top_count
    row_ids = jnp.arange(row_count, dtype=jnp.int32)
    earlier = (dest_rows[:, None] == dest_rows[None, :]) & (row_ids[None, :] < row_ids[:, None])
    rank_in = jnp.sum(earlier.astype(jnp.int32), axis=1)
    send_slot = dest_rows * capacity + rank_in
    slot_table = jnp.full((device_count * capacity,), -1, jnp.int32).at[send_slot].set(row_ids)
    is_live = slot_table >= 0
    safe_ids = jnp.maximum(slot_table, 0)
    token_ids = safe_ids // top_count
    send_x = jnp.where(is_live[:, None], tokens_in[token_ids], jnp.zeros((), tokens_in.dtype))
    send_dy = jnp.where(is_live[:, None], grad_out[token_ids], jnp.zeros((), grad_out.dtype))
    send_gate = jnp.where(
        is_live, gate_weights.reshape(-1)[safe_ids], jnp.zeros((), gate_weights.dtype)
    )
    block_shape = (group_count, lane_count, capacity, model_width)
    outgoing = (
        send_x.reshape(block_shape),
        send_dy.reshape(block_shape),
        send_gate.reshape(group_count, lane_count, capacity),
    )
    arrived = (
        lax.all_to_all(
            lax.all_to_all(outgoing[0], "ep", split_axis=1, concat_axis=1, tiled=True),
            "grp",
            split_axis=0,
            concat_axis=0,
            tiled=True,
        ),
        lax.all_to_all(
            lax.all_to_all(outgoing[1], "ep", split_axis=1, concat_axis=1, tiled=True),
            "grp",
            split_axis=0,
            concat_axis=0,
            tiled=True,
        ),
        lax.all_to_all(
            lax.all_to_all(outgoing[2], "ep", split_axis=1, concat_axis=1, tiled=True),
            "grp",
            split_axis=0,
            concat_axis=0,
            tiled=True,
        ),
    )
    rows_x = arrived[0].reshape(device_count * capacity, model_width)
    rows_dy = arrived[1].reshape(device_count * capacity, model_width)
    rows_gate = arrived[2].reshape(device_count * capacity)
    row_grad, gate_grad, part_in, part_down = expert_backward(
        rows_x, rows_dy, rows_gate, w_in, w_down
    )
    returning = (
        row_grad.reshape(block_shape),
        gate_grad.reshape(group_count, lane_count, capacity),
    )
    came_back = (
        lax.all_to_all(
            lax.all_to_all(returning[0], "grp", split_axis=0, concat_axis=0, tiled=True),
            "ep",
            split_axis=1,
            concat_axis=1,
            tiled=True,
        ),
        lax.all_to_all(
            lax.all_to_all(returning[1], "grp", split_axis=0, concat_axis=0, tiled=True),
            "ep",
            split_axis=1,
            concat_axis=1,
            tiled=True,
        ),
    )
    grads_rows = came_back[0].reshape(device_count * capacity, model_width)[send_slot]
    d_tokens = jnp.sum(
        grads_rows.reshape(tok_count, top_count, model_width).astype(jnp.float32), axis=1
    ).astype(jnp.bfloat16)
    d_gates = came_back[1].reshape(-1)[send_slot].reshape(tok_count, top_count)
    group_index = lax.axis_index("grp")
    column_index = lax.axis_index("ep")
    my_slot = placement[group_index, column_index]
    slot_mask = (jnp.arange(KPC, dtype=jnp.int32) == my_slot).astype(jnp.float32)
    stack_in = slot_mask[:, None, None] * part_in[None]
    stack_down = slot_mask[:, None, None] * part_down[None]
    summed_in, summed_down = (
        lax.psum_scatter(
            stack_in.astype(jnp.bfloat16), "grp", scatter_dimension=1, tiled=True
        ).astype(jnp.float32),
        lax.psum_scatter(
            stack_down.astype(jnp.bfloat16), "grp", scatter_dimension=1, tiled=True
        ).astype(jnp.float32),
    )
    return (d_tokens, d_gates, summed_in.astype(jnp.bfloat16), summed_down.astype(jnp.bfloat16))


def shards(tokens_in, grad_out, replica_of, gate_weights, placement, w_in_rep, w_down_rep):
    tok_count, width = tokens_in.shape
    top_count = replica_of.shape[1]
    groups = lax.axis_size("grp")
    lanes = lax.axis_size("ep")
    devices = groups * lanes
    cap = max(2, 2 * tok_count * top_count // devices)
    if cap % 16 or top_count != 2 or groups != 4:
        return plain_shards(
            tokens_in, grad_out, replica_of, gate_weights, placement, w_in_rep, w_down_rep
        )
    inner = max(1, min(lanes, tok_count // (groups * cap)))
    outer = lanes // inner
    plane = groups // 2 * inner
    senders = groups // 2 * lanes
    w_in = w_in_rep[0, 0]
    w_down = w_down_rep[0, 0]
    hidden = w_down.shape[1]
    dest_rows = replica_of.reshape(-1)
    row_ids = jnp.arange(tok_count * top_count, dtype=jnp.int32)
    earlier = (dest_rows[:, None] == dest_rows[None, :]) & (row_ids[None, :] < row_ids[:, None])
    rank_in = jnp.sum(earlier.astype(jnp.int32), axis=1).reshape(tok_count, top_count)
    first_fits = (placement[2] != placement[0]) | (placement[3] != placement[0])
    low_expert = jnp.where(first_fits, placement[0], placement[1])
    side_table = jnp.where(placement == low_expert[None, :], 0, 1)
    same = placement[:, None, :] == placement[None, :, :]
    before = jnp.arange(groups)[None, :, None] < jnp.arange(groups)[:, None, None]
    copy_table = jnp.sum((same & before).astype(jnp.int32), axis=1)
    table = (side_table * groups + copy_table).reshape(-1)
    named = replica_of[:, :, None] == jnp.arange(devices, dtype=jnp.int32)
    entry = jnp.sum(jnp.where(named, table, 0), axis=2)
    side_of = entry // groups
    spot = entry % groups * cap + rank_in
    cap = (groups - 1) * cap
    lane_of = replica_of % lanes
    seat_of = side_of * inner + lane_of % inner
    facts = jnp.concatenate(
        [
            gate_weights,
            (lane_of // inner).astype(BF16),
            (seat_of * cap + spot).astype(BF16),
            jnp.zeros((tok_count, 128 - 3 * top_count), BF16),
        ],
        axis=1,
    )
    tok = jnp.concatenate([tokens_in, grad_out, facts], axis=1)
    full = tok.shape[1]
    any_spec = pl.BlockSpec(memory_space=pl.ANY)
    vmem_spec = pl.BlockSpec(memory_space=pltpu.VMEM)
    dma = pltpu.SemaphoreType.DMA
    share = width // groups
    my_group = lax.axis_index("grp")
    my_lane = lax.axis_index("ep")
    side = my_group // 2
    my_expert = jnp.where(side == 0, low_expert[my_lane], 1 - low_expert[my_lane])
    own_fits = placement[my_group, my_lane] == my_expert
    choices = jnp.stack([own_fits, ~own_fits, my_expert == 0, my_expert == 1]).astype(F32)
    mask = jnp.broadcast_to(jnp.pad(choices, (0, 4))[:, None], (8, 128))
    batch = plane * cap
    d_tokens, gates, grad_in, grad_down = pl.pallas_call(
        functools.partial(layer_kernel, groups, lanes, inner, cap),
        out_shape=(
            jax.ShapeDtypeStruct((tok_count, width), BF16),
            jax.ShapeDtypeStruct((tok_count, 128), BF16),
            jax.ShapeDtypeStruct((KPC, share, 2 * hidden), BF16),
            jax.ShapeDtypeStruct((KPC, share, hidden), BF16),
        ),
        in_specs=[vmem_spec, vmem_spec, vmem_spec, any_spec, any_spec],
        out_specs=(vmem_spec,) * 4,
        scratch_shapes=[
            pltpu.VMEM((outer, tok_count, full), BF16),
            pltpu.VMEM((outer, plane, cap, full), BF16),
            pltpu.VMEM((outer, plane, cap, full), BF16),
            pltpu.VMEM((width, 2 * hidden), BF16),
            pltpu.VMEM((width, hidden), BF16),
            pltpu.VMEM((width, 2 * hidden), BF16),
            pltpu.VMEM((width, hidden), BF16),
            pltpu.VMEM((outer, batch, 2 * hidden), BF16),
            pltpu.VMEM((outer, batch, hidden), BF16),
            pltpu.VMEM((outer, plane, cap, width + 128), BF16),
            pltpu.VMEM((senders, cap, width + 128), BF16),
            pltpu.VMEM((2, share, 2 * hidden), BF16),
            pltpu.VMEM((2, share, hidden), BF16),
            pltpu.VMEM((2, share, 2 * hidden), BF16),
            pltpu.VMEM((2, share, hidden), BF16),
            pltpu.VMEM((share, 2 * hidden), BF16),
            pltpu.VMEM((share, hidden), BF16),
            pltpu.VMEM((share, 2 * hidden), BF16),
            pltpu.VMEM((share, hidden), BF16),
            dma((outer, PIECES)),
            dma((outer, PIECES)),
            dma((outer, PIECES)),
            dma((outer, plane)),
            dma((outer, plane)),
            dma((outer,)),
            dma((2,)),
            dma((outer, plane)),
            dma((senders,)),
            dma,
            dma((2,)),
            dma((2,)),
            dma((2, 2)),
            dma((2, 2)),
            dma((2,)),
            dma((2,)),
        ],
        compiler_params=pltpu.CompilerParams(
            collective_id=0, has_side_effects=True, vmem_limit_bytes=58 * 2**20
        ),
        name="layer_backward",
    )(tok, (side_of * lanes + lane_of) * cap + spot, mask, w_in, w_down)
    return d_tokens, gates[:, :top_count], grad_in, grad_down


def solution(mesh):
    placed = (
        P(("grp", "ep"), None),
        P(("grp", "ep"), None),
        P(("grp", "ep"), None),
        P(("grp", "ep"), None),
        P(),
        P("grp", "ep", None, None),
        P("grp", "ep", None, None),
    )
    return jax.shard_map(
        shards,
        mesh=mesh,
        in_specs=placed,
        out_specs=(
            P(("grp", "ep"), None),
            P(("grp", "ep"), None),
            P("ep", "grp", None),
            P("ep", "grp", None),
        ),
        check_vma=False,
    )
```

```python
import functools

import jax
import jax.numpy as jnp
from jax import lax
from jax.experimental import pallas as pl
from jax.experimental.pallas import tpu as pltpu
from jax.sharding import PartitionSpec as P

KPC = 2
MESH = pl.DeviceIdType.MESH
F32 = jnp.float32
BF16 = jnp.bfloat16
PIECES = 5


def layer_kernel(groups, lanes, inner, cap, x_ref, dy_ref, routes_ref, copies_ref,
                 w_in_hbm, w_down_hbm,
                 tokens_ref, gates_ref, grad_in_ref, grad_down_ref,
                 held_facts, held_x, held_dy, picked_x, picked_dy, rows_x, rows_dy, marks, flags,
                 w_in, w_down, other_in, other_down,
                 both_grads, gated, row_grads, back,
                 sib_in, sib_down, from_in, from_down, cross_in, cross_down, got_in, got_down,
                 up_send, down_send, chain_recv, plane_send, plane_recv, own_sem, load_sem,
                 row_send, row_recv, row_own, swap_send, swap_recv, sib_send, sib_recv,
                 cross_send, cross_recv):
    tok_count, width = x_ref.shape
    full = width + 128
    rows_each = cap
    cap = (groups - 1) * cap
    hidden = w_down.shape[1]
    outer = lanes // inner
    plane = groups // 2 * inner
    devices = groups * lanes
    batch = plane * cap
    senders = groups // 2 * lanes
    share = width // groups
    my_group = lax.axis_index("grp")
    my_lane = lax.axis_index("ep")
    me = my_group * lanes + my_lane
    layer = my_lane // inner
    side = my_group // 2
    core = lax.rem(my_group, 2)
    my_seat = side * inner + lax.rem(my_lane, inner)
    my_sender = side * lanes + my_lane
    sibling = (side * 2 + 1 - core, my_lane)
    across = ((1 - side) * 2 + core, my_lane)
    half = tok_count // 2

    load_in = pltpu.make_async_copy(w_in_hbm, w_in, load_sem.at[0])
    load_down = pltpu.make_async_copy(w_down_hbm, w_down, load_sem.at[1])
    load_in.start()
    load_down.start()

    barrier = pltpu.get_barrier_semaphore()

    @pl.loop(1, devices)
    def _(off):
        peer = lax.rem(me + off, devices)
        pl.semaphore_signal(barrier, inc=1, device_id=(peer // lanes, lax.rem(peer, lanes)),
                            device_id_type=MESH)

    pl.semaphore_wait(barrier, devices - 1)

    def remote(src, dst, send, recv, device):
        return pltpu.make_async_remote_copy(
            src_ref=src, dst_ref=dst, send_sem=send, recv_sem=recv,
            device_id=device, device_id_type=MESH)

    swaps = [
        remote(w_in_hbm, other_in, swap_send.at[0], swap_recv.at[0], sibling),
        remote(w_down_hbm, other_down, swap_send.at[1], swap_recv.at[1], sibling),
    ]
    for swap in swaps:
        swap.start()

    device_ids = lax.broadcasted_iota(jnp.int32, (1, 128), 1)
    group_ids = device_ids // lanes
    lane_in = device_ids - group_ids * lanes
    copies = [copies_ref[group:group + 1] for group in range(groups)]
    low = jnp.where((copies[2] != copies[0]) | (copies[3] != copies[0]), copies[0], copies[1])
    mine = sum(jnp.where(group_ids == group, copies[group], 0.0) for group in range(groups))
    side_table = (mine != low).astype(F32)
    copy_table = sum(
        ((copies[group] == mine) & (group_ids > group)).astype(F32) for group in range(groups))
    layer_table = (lane_in // inner).astype(F32)
    within_table = lax.rem(lane_in, inner).astype(F32)
    copy_base = copy_table * rows_each
    place_table = (side_table * inner + within_table) * cap + copy_base
    back_table = (side_table * lanes + lane_in.astype(F32)) * cap + copy_base
    here_only = device_ids == me
    my_low = jnp.sum(jnp.where(here_only, low, 0.0), axis=1, keepdims=True)
    my_held = jnp.sum(jnp.where(here_only, mine, 0.0), axis=1, keepdims=True)
    on_high = side.astype(F32)
    my_expert = my_low * (1.0 - on_high) + (1.0 - my_low) * on_high
    flags[0:1] = jnp.broadcast_to((my_held == my_expert).astype(F32), (1, 128))
    flags[1:2] = jnp.broadcast_to((my_held != my_expert).astype(F32), (1, 128))
    flags[2:3] = jnp.broadcast_to(1.0 - my_expert, (1, 128))
    flags[3:4] = jnp.broadcast_to(my_expert, (1, 128))
    routes = routes_ref[...]
    across_tokens = routes.T
    token_ids = lax.broadcasted_iota(jnp.int32, (tok_count, tok_count), 0)
    other_ids = lax.broadcasted_iota(jnp.int32, (tok_count, tok_count), 1)
    earlier = other_ids < token_ids
    column_ids = lax.broadcasted_iota(jnp.int32, (tok_count, 128), 1)
    spread_ids = column_ids.astype(F32)
    facts = jnp.where(column_ids < 2, pltpu.roll(routes, 126, 1), 0.0)
    backs = jnp.zeros((tok_count, 128), F32)
    for k in range(2):
        named = routes[:, k:k + 1]
        same = (named == across_tokens[0:1]).astype(F32) + (named == across_tokens[1:2]).astype(F32)
        rank = jnp.sum(jnp.where(earlier, same, 0.0), axis=1, keepdims=True)
        chosen = named == spread_ids

        def look(table):
            return jnp.sum(jnp.where(chosen, table, 0.0), axis=1, keepdims=True)

        facts = jnp.where(column_ids == 2 + k, look(layer_table), facts)
        facts = jnp.where(column_ids == 4 + k, look(place_table) + rank, facts)
        backs = jnp.where(column_ids == k, look(back_table) + rank, backs)
    held_facts[layer] = facts.astype(BF16)
    marks[...] = backs

    def hop(source, part, upward, own):
        if part == 0:
            src = dst = held_facts.at[source]
        else:
            box, given = (held_x, x_ref) if part < 3 else (held_dy, dy_ref)
            at = pl.ds((part - 1) % 2 * half, half)
            dst = box.at[source, at]
            src = given.at[at] if own else dst
        sems = up_send if upward else down_send
        return remote(src, dst, sems.at[source, part], chain_recv.at[source, part],
                      (my_group, my_lane + inner if upward else my_lane - inner))

    boxes = ((picked_x, rows_x), (picked_dy, rows_dy))

    def spread(source, off, kind):
        seat = lax.rem(my_seat + off, plane)
        src, dst = boxes[kind]
        return remote(src.at[source, seat], dst.at[source, my_seat],
                      plane_send.at[kind, source, off], plane_recv.at[kind, source, off],
                      (seat // inner * 2 + core, layer * inner + lax.rem(seat, inner)))

    def own_copy(source, kind):
        src, dst = boxes[kind]
        return pltpu.make_async_copy(
            src.at[source, my_seat], dst.at[source, my_seat], own_sem.at[kind, source])

    def row_copy(source, seat):
        return pltpu.make_async_remote_copy(
            src_ref=row_grads.at[source, seat],
            dst_ref=back.at[my_sender],
            send_sem=row_send.at[source, seat],
            recv_sem=row_recv.at[my_sender],
            device_id=(seat // inner * 2 + core, source * inner + lax.rem(seat, inner)),
            device_id_type=MESH,
        )

    def row_arrival(peer):
        return pltpu.make_async_remote_copy(
            src_ref=row_grads.at[0, 0],
            dst_ref=back.at[peer],
            send_sem=row_send.at[0, 0],
            recv_sem=row_recv.at[peer],
            device_id=(peer // lanes * 2 + core, lax.rem(peer, lanes)),
            device_id_type=MESH,
        )

    row_stay = pltpu.make_async_copy(row_grads.at[layer, my_seat], back.at[my_sender], row_own)

    def pick(source, view, kind):
        facts = held_facts[source].astype(F32).T
        slots = lax.broadcasted_iota(jnp.int32, (batch, tok_count), 0).astype(F32)
        here = layer.astype(F32)
        first = ((facts[2:3] == here) & (facts[4:5] == slots)).astype(F32)
        second = ((facts[3:4] == here) & (facts[5:6] == slots)).astype(F32)
        chosen = (first + second).astype(BF16)
        step = 1024
        picked = boxes[kind][0]
        for begin in range(0, width, step):
            got = jnp.dot(chosen, view[:, begin:begin + step], preferred_element_type=F32)
            picked[source, :, :, begin:begin + step] = got.astype(BF16).reshape(plane, cap, step)
        if kind == 0:
            weights = jnp.sum(first * facts[0:1] + second * facts[1:2], axis=1, keepdims=True)
            tail = jnp.broadcast_to(weights, (batch, 128)).astype(BF16)
            picked[source, :, :, width:] = tail.reshape(plane, cap, 128)
        own_copy(source, kind).start()

        @pl.loop(1, plane)
        def _(off):
            spread(source, off, kind).start()

    def arrive(source, kind):
        own_copy(source, kind).wait()

        @pl.loop(1, plane)
        def _(off):
            spread(source, off, kind).wait_recv()

    def work(source):
        arrive(source, 0)
        row_x = rows_x[source, :, :, :width].reshape(batch, width)
        weight = rows_x[source, :, :, width:].reshape(batch, 128)[:, :1].astype(F32)
        both = jnp.dot(row_x, w_in[...], preferred_element_type=F32)
        arrive(source, 1)
        row_dy = rows_dy[source].reshape(batch, width)
        back_act = jnp.dot(row_dy, w_down[...], preferred_element_type=F32)
        gate_pre = both[:, :hidden]
        up_part = both[:, hidden:]
        sig = jax.nn.sigmoid(gate_pre)
        silu = gate_pre * sig
        act = silu * up_part
        gate_grad = jnp.sum(act * back_act, axis=1, keepdims=True)
        act_grad = weight * back_act
        gated[source] = (weight * act).astype(BF16)
        gate_side = act_grad * up_part * sig * (1.0 + gate_pre * (1.0 - sig))
        both_grads[source, :, :hidden] = gate_side.astype(BF16)
        both_grads[source, :, hidden:] = (act_grad * silu).astype(BF16)
        step = 512
        for begin in range(0, width, step):
            got = lax.dot_general(
                both_grads[source], w_in[begin:begin + step, :], (((1,), (1,)), ((), ())),
                preferred_element_type=F32)
            row_grads[source, :, :, begin:begin + step] = got.astype(BF16).reshape(
                plane, cap, step)
        row_grads[source, :, :, width:] = jnp.broadcast_to(gate_grad, (batch, 128)).astype(
            BF16).reshape(plane, cap, 128)

        @pl.loop(0, plane)
        def _(seat):
            mine = (source == layer) & (seat == my_seat)

            @pl.when(mine)
            def _():
                row_stay.start()

            @pl.when(jnp.logical_not(mine))
            def _():
                row_copy(source, seat).start()

    for part in range(PIECES):
        @pl.when(layer < outer - 1)
        def _():
            hop(layer, part, True, True).start()

        @pl.when(layer > 0)
        def _():
            hop(layer, part, False, True).start()
    pick(layer, x_ref, 0)
    pick(layer, dy_ref, 1)

    @pl.loop(1, outer + 1)
    def _(far):
        below = layer - far
        above = layer + far

        @pl.when(far < outer)
        def _():
            for kind, parts, box in ((0, (0, 1, 2), held_x), (1, (3, 4), held_dy)):
                for part in parts:
                    @pl.when(below >= 0)
                    def _():
                        hop(below, part, True, False).wait_recv()

                        @pl.when(layer < outer - 1)
                        def _():
                            hop(below, part, True, False).start()

                    @pl.when(above < outer)
                    def _():
                        hop(above, part, False, False).wait_recv()

                        @pl.when(layer > 0)
                        def _():
                            hop(above, part, False, False).start()

                @pl.loop(0, 2)
                def _(way):
                    source = layer + (2 * way - 1) * far

                    @pl.when((source >= 0) & (source < outer))
                    def _():
                        pick(source, box.at[source], kind)

        @pl.when(far == 1)
        def _():
            load_in.wait()
            load_down.wait()
            for swap in swaps:
                swap.wait()

            @pl.loop(0, width // 64)
            def _(i):
                at = pl.ds(pl.multiple_of(i * 64, 64), 64)
                own = flags[0:1, :1].astype(BF16)
                theirs = flags[1:2, :1].astype(BF16)
                w_in[at] = own * w_in[at] + theirs * other_in[at]
                w_down[at] = own * w_down[at] + theirs * other_down[at]

        @pl.loop(0, 2)
        def _(way):
            source = layer + (2 * way - 1) * (far - 1)

            @pl.when((source >= 0) & (source < outer) & (far + way > 1))
            def _():
                work(source)

    total = outer * batch
    grads = both_grads[...].reshape(total, 2 * hidden)
    acts = gated[...].reshape(total, hidden)

    def part_of(group, box, other):
        columns = pl.ds(pl.multiple_of(group * share, share), share)
        some = box[:, :, :, columns].reshape(total, share)
        return lax.dot_general(some, other, (((0,), (0,)), ((), ())), preferred_element_type=F32)

    kinds = (
        (rows_x, grads, sib_in, from_in, cross_in, got_in, grad_in_ref),
        (rows_dy, acts, sib_down, from_down, cross_down, got_down, grad_down_ref),
    )

    def to_sibling(kind, which):
        return remote(kinds[kind][2].at[which], kinds[kind][3].at[which],
                      sib_send.at[kind, which], sib_recv.at[kind, which], sibling)

    def to_across(kind):
        return remote(kinds[kind][4], kinds[kind][5], cross_send.at[kind], cross_recv.at[kind],
                      across)

    for which, target in ((0, 1 - side), (1, side)):
        for kind in range(2):
            box, other, sib = kinds[kind][:3]
            sib[which] = part_of(target * 2 + 1 - core, box, other).astype(BF16)
            to_sibling(kind, which).start()
        for kind in range(2):
            box, other, _, arrived, crossing, _, out = kinds[kind]
            mine = part_of(target * 2 + core, box, other)
            to_sibling(kind, which).wait_recv()
            joined = (mine + arrived[which].astype(F32)).astype(BF16)
            if which == 0:
                crossing[...] = joined
                to_across(kind).start()
            else:
                out[0] = joined

    row_stay.wait()

    @pl.loop(1, senders)
    def _(off):
        row_arrival(lax.rem(my_sender + off, senders)).wait_recv()

    places = lax.broadcasted_iota(jnp.int32, (tok_count, senders * cap), 1).astype(F32)
    first = (marks[:, 0:1] == places).astype(F32)
    second = (marks[:, 1:2] == places).astype(F32)
    chosen = (first + second).astype(BF16)
    for begin in range(0, width, 512):
        view = back[:, :, begin:begin + 512].reshape(senders * cap, 512)
        tokens_ref[:, begin:begin + 512] = jnp.dot(
            chosen, view, preferred_element_type=F32).astype(BF16)
    tail = back[:, :, width:].reshape(senders * cap, 128)
    gate_first = jnp.dot(first.astype(BF16), tail, preferred_element_type=F32)
    gate_second = jnp.dot(second.astype(BF16), tail, preferred_element_type=F32)
    lane_ids = lax.broadcasted_iota(jnp.int32, (tok_count, 128), 1)
    gates_ref[...] = jnp.where(lane_ids == 0, gate_first, gate_second).astype(BF16)

    for kind in range(2):
        to_across(kind).wait()
        to_sibling(kind, 0).wait_send()
        to_sibling(kind, 1).wait_send()

    @pl.loop(0, share // 16)
    def _(i):
        at = pl.ds(pl.multiple_of(i * 16, 16), 16)
        for kind in range(2):
            got, out = kinds[kind][5:]
            near = out[0, at].astype(F32)
            away = got[at].astype(F32)
            lower = flags[2:3, :1]
            upper = flags[3:4, :1]
            out[0, at] = (lower * near + upper * away).astype(BF16)
            out[1, at] = (upper * near + lower * away).astype(BF16)

    for source in range(outer):
        @pl.loop(1, plane)
        def _(off):
            spread(source, off, 0).wait_send()
            spread(source, off, 1).wait_send()

        @pl.loop(0, plane)
        def _(seat):
            @pl.when(jnp.logical_not((source == layer) & (seat == my_seat)))
            def _():
                row_copy(source, seat).wait_send()

        for part in range(PIECES):
            @pl.when((source <= layer) & (layer < outer - 1))
            def _():
                hop(source, part, True, False).wait_send()

            @pl.when((source >= layer) & (layer > 0))
            def _():
                hop(source, part, False, False).wait_send()


def expert_backward(rows_x, rows_dy, rows_gate, w_in, w_down):
    hidden = w_down.shape[1]
    both = jnp.dot(rows_x, w_in, preferred_element_type=jnp.float32)
    gate_pre = both[:, :hidden]
    up_part = both[:, hidden:]
    sigmoid_gate = jax.nn.sigmoid(gate_pre)
    silu_gate = gate_pre * sigmoid_gate
    activation = (silu_gate * up_part).astype(jnp.bfloat16)
    out_rows = lax.dot_general(
        activation, w_down, (((1,), (1,)), ((), ())), preferred_element_type=jnp.float32
    )
    gate_grad = jnp.sum(rows_dy.astype(jnp.float32) * out_rows, axis=1).astype(jnp.bfloat16)
    out_grad = (rows_gate.astype(jnp.float32)[:, None] * rows_dy.astype(jnp.float32)).astype(
        jnp.bfloat16
    )
    act_grad = jnp.dot(out_grad, w_down, preferred_element_type=jnp.float32)
    gate_grad_pre = act_grad * up_part * sigmoid_gate * (1.0 + gate_pre * (1.0 - sigmoid_gate))
    up_grad = act_grad * silu_gate
    both_grad = jnp.concatenate([gate_grad_pre, up_grad], axis=1).astype(jnp.bfloat16)
    row_grad = lax.dot_general(
        both_grad, w_in, (((1,), (1,)), ((), ())), preferred_element_type=jnp.float32
    ).astype(jnp.bfloat16)
    part_in = lax.dot_general(
        rows_x, both_grad, (((0,), (0,)), ((), ())), preferred_element_type=jnp.float32
    )
    part_down = lax.dot_general(
        out_grad, activation, (((0,), (0,)), ((), ())), preferred_element_type=jnp.float32
    )
    return (row_grad, gate_grad, part_in, part_down)


def plain_shards(tokens_in, grad_out, replica_of, gate_weights, placement, w_in_rep, w_down_rep):
    tok_count, model_width = tokens_in.shape
    top_count = replica_of.shape[1]
    group_count = lax.axis_size("grp")
    lane_count = lax.axis_size("ep")
    device_count = group_count * lane_count
    capacity = max(2, 2 * tok_count * top_count // device_count)
    w_in = w_in_rep[0, 0]
    w_down = w_down_rep[0, 0]
    dest_rows = replica_of.reshape(-1)
    row_count = tok_count * top_count
    row_ids = jnp.arange(row_count, dtype=jnp.int32)
    earlier = (dest_rows[:, None] == dest_rows[None, :]) & (row_ids[None, :] < row_ids[:, None])
    rank_in = jnp.sum(earlier.astype(jnp.int32), axis=1)
    send_slot = dest_rows * capacity + rank_in
    slot_table = jnp.full((device_count * capacity,), -1, jnp.int32).at[send_slot].set(row_ids)
    is_live = slot_table >= 0
    safe_ids = jnp.maximum(slot_table, 0)
    token_ids = safe_ids // top_count
    send_x = jnp.where(is_live[:, None], tokens_in[token_ids], jnp.zeros((), tokens_in.dtype))
    send_dy = jnp.where(is_live[:, None], grad_out[token_ids], jnp.zeros((), grad_out.dtype))
    send_gate = jnp.where(
        is_live, gate_weights.reshape(-1)[safe_ids], jnp.zeros((), gate_weights.dtype)
    )
    block_shape = (group_count, lane_count, capacity, model_width)
    outgoing = (
        send_x.reshape(block_shape),
        send_dy.reshape(block_shape),
        send_gate.reshape(group_count, lane_count, capacity),
    )
    arrived = (
        lax.all_to_all(
            lax.all_to_all(outgoing[0], "ep", split_axis=1, concat_axis=1, tiled=True),
            "grp",
            split_axis=0,
            concat_axis=0,
            tiled=True,
        ),
        lax.all_to_all(
            lax.all_to_all(outgoing[1], "ep", split_axis=1, concat_axis=1, tiled=True),
            "grp",
            split_axis=0,
            concat_axis=0,
            tiled=True,
        ),
        lax.all_to_all(
            lax.all_to_all(outgoing[2], "ep", split_axis=1, concat_axis=1, tiled=True),
            "grp",
            split_axis=0,
            concat_axis=0,
            tiled=True,
        ),
    )
    rows_x = arrived[0].reshape(device_count * capacity, model_width)
    rows_dy = arrived[1].reshape(device_count * capacity, model_width)
    rows_gate = arrived[2].reshape(device_count * capacity)
    row_grad, gate_grad, part_in, part_down = expert_backward(
        rows_x, rows_dy, rows_gate, w_in, w_down
    )
    returning = (
        row_grad.reshape(block_shape),
        gate_grad.reshape(group_count, lane_count, capacity),
    )
    came_back = (
        lax.all_to_all(
            lax.all_to_all(returning[0], "grp", split_axis=0, concat_axis=0, tiled=True),
            "ep",
            split_axis=1,
            concat_axis=1,
            tiled=True,
        ),
        lax.all_to_all(
            lax.all_to_all(returning[1], "grp", split_axis=0, concat_axis=0, tiled=True),
            "ep",
            split_axis=1,
            concat_axis=1,
            tiled=True,
        ),
    )
    grads_rows = came_back[0].reshape(device_count * capacity, model_width)[send_slot]
    d_tokens = jnp.sum(
        grads_rows.reshape(tok_count, top_count, model_width).astype(jnp.float32), axis=1
    ).astype(jnp.bfloat16)
    d_gates = came_back[1].reshape(-1)[send_slot].reshape(tok_count, top_count)
    group_index = lax.axis_index("grp")
    column_index = lax.axis_index("ep")
    my_slot = placement[group_index, column_index]
    slot_mask = (jnp.arange(KPC, dtype=jnp.int32) == my_slot).astype(jnp.float32)
    stack_in = slot_mask[:, None, None] * part_in[None]
    stack_down = slot_mask[:, None, None] * part_down[None]
    summed_in, summed_down = (
        lax.psum_scatter(
            stack_in.astype(jnp.bfloat16), "grp", scatter_dimension=1, tiled=True
        ).astype(jnp.float32),
        lax.psum_scatter(
            stack_down.astype(jnp.bfloat16), "grp", scatter_dimension=1, tiled=True
        ).astype(jnp.float32),
    )
    return (d_tokens, d_gates, summed_in.astype(jnp.bfloat16), summed_down.astype(jnp.bfloat16))


def shards(tokens_in, grad_out, replica_of, gate_weights, placement, w_in_rep, w_down_rep):
    tok_count, width = tokens_in.shape
    top_count = replica_of.shape[1]
    groups = lax.axis_size("grp")
    lanes = lax.axis_size("ep")
    devices = groups * lanes
    cap = max(2, 2 * tok_count * top_count // devices)
    if cap % 16 or top_count != 2 or groups != 4:
        return plain_shards(
            tokens_in, grad_out, replica_of, gate_weights, placement, w_in_rep, w_down_rep
        )
    inner = max(1, min(lanes, tok_count // (groups * cap)))
    outer = lanes // inner
    plane = groups // 2 * inner
    senders = groups // 2 * lanes
    w_in = w_in_rep[0, 0]
    w_down = w_down_rep[0, 0]
    hidden = w_down.shape[1]
    routes = jnp.concatenate(
        [
            replica_of.astype(F32),
            gate_weights.astype(F32),
            jnp.zeros((tok_count, 128 - 2 * top_count), F32),
        ],
        axis=1,
    )
    copies = jnp.pad(
        jnp.tile(placement, (1, groups)).astype(F32), ((0, 8 - groups), (0, 128 - devices))
    )
    rows_each = cap
    cap = (groups - 1) * cap
    full = width + 128
    any_spec = pl.BlockSpec(memory_space=pl.ANY)
    vmem_spec = pl.BlockSpec(memory_space=pltpu.VMEM)
    dma = pltpu.SemaphoreType.DMA
    share = width // groups
    batch = plane * cap
    d_tokens, gates, grad_in, grad_down = pl.pallas_call(
        functools.partial(layer_kernel, groups, lanes, inner, rows_each),
        out_shape=(
            jax.ShapeDtypeStruct((tok_count, width), BF16),
            jax.ShapeDtypeStruct((tok_count, 128), BF16),
            jax.ShapeDtypeStruct((KPC, share, 2 * hidden), BF16),
            jax.ShapeDtypeStruct((KPC, share, hidden), BF16),
        ),
        in_specs=[vmem_spec] * 4 + [any_spec] * 2,
        out_specs=(vmem_spec,) * 4,
        scratch_shapes=[
            pltpu.VMEM((outer, tok_count, 128), BF16),
            pltpu.VMEM((outer, tok_count, width), BF16),
            pltpu.VMEM((outer, tok_count, width), BF16),
            pltpu.VMEM((outer, plane, cap, full), BF16),
            pltpu.VMEM((outer, plane, cap, width), BF16),
            pltpu.VMEM((outer, plane, cap, full), BF16),
            pltpu.VMEM((outer, plane, cap, width), BF16),
            pltpu.VMEM((tok_count, 128), F32),
            pltpu.VMEM((8, 128), F32),
            pltpu.VMEM((width, 2 * hidden), BF16),
            pltpu.VMEM((width, hidden), BF16),
            pltpu.VMEM((width, 2 * hidden), BF16),
            pltpu.VMEM((width, hidden), BF16),
            pltpu.VMEM((outer, batch, 2 * hidden), BF16),
            pltpu.VMEM((outer, batch, hidden), BF16),
            pltpu.VMEM((outer, plane, cap, width + 128), BF16),
            pltpu.VMEM((senders, cap, width + 128), BF16),
            pltpu.VMEM((2, share, 2 * hidden), BF16),
            pltpu.VMEM((2, share, hidden), BF16),
            pltpu.VMEM((2, share, 2 * hidden), BF16),
            pltpu.VMEM((2, share, hidden), BF16),
            pltpu.VMEM((share, 2 * hidden), BF16),
            pltpu.VMEM((share, hidden), BF16),
            pltpu.VMEM((share, 2 * hidden), BF16),
            pltpu.VMEM((share, hidden), BF16),
            dma((outer, PIECES)),
            dma((outer, PIECES)),
            dma((outer, PIECES)),
            dma((2, outer, plane)),
            dma((2, outer, plane)),
            dma((2, outer)),
            dma((2,)),
            dma((outer, plane)),
            dma((senders,)),
            dma,
            dma((2,)),
            dma((2,)),
            dma((2, 2)),
            dma((2, 2)),
            dma((2,)),
            dma((2,)),
        ],
        compiler_params=pltpu.CompilerParams(
            collective_id=0, has_side_effects=True, vmem_limit_bytes=58 * 2**20
        ),
        name="layer_backward",
    )(tokens_in, grad_out, routes, copies, w_in, w_down)
    return d_tokens, gates[:, :top_count], grad_in, grad_down


def solution(mesh):
    placed = (
        P(("grp", "ep"), None),
        P(("grp", "ep"), None),
        P(("grp", "ep"), None),
        P(("grp", "ep"), None),
        P(),
        P("grp", "ep", None, None),
        P("grp", "ep", None, None),
    )
    return jax.shard_map(
        shards,
        mesh=mesh,
        in_specs=placed,
        out_specs=(
            P(("grp", "ep"), None),
            P(("grp", "ep"), None),
            P("ep", "grp", None),
            P("ep", "grp", None),
        ),
        check_vma=False,
    )
```

```python
import functools

import jax
import jax.numpy as jnp
from jax import lax
from jax.experimental import pallas as pl
from jax.experimental.pallas import tpu as pltpu
from jax.sharding import PartitionSpec as P

KPC = 2
MESH = pl.DeviceIdType.MESH
F32 = jnp.float32
BF16 = jnp.bfloat16
PIECES = 5


def layer_kernel(groups, lanes, inner, cap, x_ref, dy_ref, routes_ref, copies_ref,
                 w_in_hbm, w_down_hbm,
                 tokens_ref, gates_ref, grad_in_ref, grad_down_ref,
                 held_facts, held_x, held_dy, picked_x, picked_dy, rows_x, rows_dy, marks, far_marks, flags,
                 near_sums, far_sums, got_sums,
                 w_in, w_down, other_in, other_down,
                 both_grads, gated, row_grads, back,
                 sib_in, sib_down, from_in, from_down, cross_in, cross_down, got_in, got_down,
                 up_send, down_send, chain_recv, plane_send, plane_recv, own_sem, load_sem,
                 row_send, row_recv, row_own, swap_send, swap_recv, sib_send, sib_recv,
                 cross_send, cross_recv, side_send, side_recv):
    tok_count, width = x_ref.shape
    full = width + 128
    rows_each = cap
    cap = (groups - 1) * cap
    hidden = w_down.shape[1]
    outer = lanes // inner
    plane = groups // 2 * inner
    devices = groups * lanes
    batch = plane * cap
    senders = groups // 2 * lanes
    share = width // groups
    my_group = lax.axis_index("grp")
    my_lane = lax.axis_index("ep")
    me = my_group * lanes + my_lane
    layer = my_lane // inner
    side = my_group // 2
    core = lax.rem(my_group, 2)
    my_seat = side * inner + lax.rem(my_lane, inner)
    my_within = lax.rem(my_lane, inner)
    sibling = (side * 2 + 1 - core, my_lane)
    across = ((1 - side) * 2 + core, my_lane)
    half = tok_count // 2

    load_in = pltpu.make_async_copy(w_in_hbm, w_in, load_sem.at[0])
    load_down = pltpu.make_async_copy(w_down_hbm, w_down, load_sem.at[1])
    load_in.start()
    load_down.start()

    barrier = pltpu.get_barrier_semaphore()

    @pl.loop(1, devices)
    def _(off):
        peer = lax.rem(me + off, devices)
        pl.semaphore_signal(barrier, inc=1, device_id=(peer // lanes, lax.rem(peer, lanes)),
                            device_id_type=MESH)

    pl.semaphore_wait(barrier, devices - 1)

    def remote(src, dst, send, recv, device):
        return pltpu.make_async_remote_copy(
            src_ref=src, dst_ref=dst, send_sem=send, recv_sem=recv,
            device_id=device, device_id_type=MESH)

    swaps = [
        remote(w_in_hbm, other_in, swap_send.at[0], swap_recv.at[0], sibling),
        remote(w_down_hbm, other_down, swap_send.at[1], swap_recv.at[1], sibling),
    ]
    for swap in swaps:
        swap.start()

    device_ids = lax.broadcasted_iota(jnp.int32, (1, 128), 1)
    group_ids = device_ids // lanes
    lane_in = device_ids - group_ids * lanes
    copies = [copies_ref[group:group + 1] for group in range(groups)]
    low = jnp.where((copies[2] != copies[0]) | (copies[3] != copies[0]), copies[0], copies[1])
    mine = sum(jnp.where(group_ids == group, copies[group], 0.0) for group in range(groups))
    side_table = (mine != low).astype(F32)
    copy_table = sum(
        ((copies[group] == mine) & (group_ids > group)).astype(F32) for group in range(groups))
    layer_table = (lane_in // inner).astype(F32)
    within_table = lax.rem(lane_in, inner).astype(F32)
    copy_base = copy_table * rows_each
    place_table = (side_table * inner + within_table) * cap + copy_base
    back_table = (side_table * lanes + lane_in.astype(F32)) * cap + copy_base
    here_only = device_ids == me
    my_low = jnp.sum(jnp.where(here_only, low, 0.0), axis=1, keepdims=True)
    my_held = jnp.sum(jnp.where(here_only, mine, 0.0), axis=1, keepdims=True)
    on_high = side.astype(F32)
    my_expert = my_low * (1.0 - on_high) + (1.0 - my_low) * on_high
    flags[0:1] = jnp.broadcast_to((my_held == my_expert).astype(F32), (1, 128))
    flags[1:2] = jnp.broadcast_to((my_held != my_expert).astype(F32), (1, 128))
    flags[2:3] = jnp.broadcast_to(1.0 - my_expert, (1, 128))
    flags[3:4] = jnp.broadcast_to(my_expert, (1, 128))
    routes = routes_ref[...]
    across_tokens = routes.T
    token_ids = lax.broadcasted_iota(jnp.int32, (tok_count, tok_count), 0)
    other_ids = lax.broadcasted_iota(jnp.int32, (tok_count, tok_count), 1)
    earlier = other_ids < token_ids
    column_ids = lax.broadcasted_iota(jnp.int32, (tok_count, 128), 1)
    spread_ids = column_ids.astype(F32)
    facts = jnp.where(column_ids < 2, pltpu.roll(routes, 126, 1), 0.0)
    backs = jnp.zeros((tok_count, 128), F32)
    for k in range(2):
        named = routes[:, k:k + 1]
        same = (named == across_tokens[0:1]).astype(F32) + (named == across_tokens[1:2]).astype(F32)
        rank = jnp.sum(jnp.where(earlier, same, 0.0), axis=1, keepdims=True)
        chosen = named == spread_ids

        def look(table):
            return jnp.sum(jnp.where(chosen, table, 0.0), axis=1, keepdims=True)

        facts = jnp.where(column_ids == 2 + k, look(layer_table), facts)
        facts = jnp.where(column_ids == 4 + k, look(place_table) + rank, facts)
        backs = jnp.where(column_ids == k, look(back_table) + rank, backs)
    held_facts[layer] = facts.astype(BF16)
    marks[...] = backs
    swap_marks = remote(marks, far_marks, side_send.at[0], side_recv.at[0], across)
    swap_marks.start()

    def hop(source, part, upward, own):
        if part == 0:
            src = dst = held_facts.at[source]
        else:
            box, given = (held_x, x_ref) if part < 3 else (held_dy, dy_ref)
            at = pl.ds((part - 1) % 2 * half, half)
            dst = box.at[source, at]
            src = given.at[at] if own else dst
        sems = up_send if upward else down_send
        return remote(src, dst, sems.at[source, part], chain_recv.at[source, part],
                      (my_group, my_lane + inner if upward else my_lane - inner))

    boxes = ((picked_x, rows_x), (picked_dy, rows_dy))

    def spread(source, off, kind):
        seat = lax.rem(my_seat + off, plane)
        src, dst = boxes[kind]
        return remote(src.at[source, seat], dst.at[source, my_seat],
                      plane_send.at[kind, source, off], plane_recv.at[kind, source, off],
                      (seat // inner * 2 + core, layer * inner + lax.rem(seat, inner)))

    def own_copy(source, kind):
        src, dst = boxes[kind]
        return pltpu.make_async_copy(
            src.at[source, my_seat], dst.at[source, my_seat], own_sem.at[kind, source])

    def row_copy(source, seat):
        slot = seat // inner * lanes + my_lane
        return remote(row_grads.at[source, seat], back.at[slot], row_send.at[source, seat],
                      row_recv.at[slot], (my_group, source * inner + lax.rem(seat, inner)))

    def row_arrival(slot):
        return remote(row_grads.at[0, 0], back.at[slot], row_send.at[0, 0], row_recv.at[slot],
                      (my_group, lax.rem(slot, lanes)))

    def row_stay(which):
        return pltpu.make_async_copy(
            row_grads.at[layer, which * inner + my_within],
            back.at[which * lanes + my_lane], row_own.at[which])

    def stays(source, seat):
        return (source == layer) & (lax.rem(seat, inner) == my_within)

    swap_sums = remote(far_sums, got_sums, side_send.at[1], side_recv.at[1], across)

    def combine(which, places_of, out):
        row_stay(which).wait()

        @pl.loop(1, lanes)
        def _(off):
            row_arrival(which * lanes + lax.rem(my_lane + off, lanes)).wait_recv()

        places = lax.broadcasted_iota(jnp.int32, (tok_count, lanes * cap), 1).astype(F32)
        places = places + (side * lanes * cap).astype(F32)
        first = (places_of[:, 0:1] == places).astype(F32)
        second = (places_of[:, 1:2] == places).astype(F32)
        chosen = (first + second).astype(BF16)
        slots = pl.ds(which * lanes, lanes)
        for begin in range(0, width, 512):
            view = back[slots, :, begin:begin + 512].reshape(lanes * cap, 512)
            out[:, begin:begin + 512] = jnp.dot(
                chosen, view, preferred_element_type=F32).astype(BF16)
        tail = back[slots, :, width:].reshape(lanes * cap, 128)
        gate_first = jnp.dot(first.astype(BF16), tail, preferred_element_type=F32)
        gate_second = jnp.dot(second.astype(BF16), tail, preferred_element_type=F32)
        lane_ids = lax.broadcasted_iota(jnp.int32, (tok_count, 128), 1)
        out[:, width:] = jnp.where(lane_ids == 0, gate_first, gate_second).astype(BF16)

    def pick(source, view, kind):
        facts = held_facts[source].astype(F32).T
        slots = lax.broadcasted_iota(jnp.int32, (batch, tok_count), 0).astype(F32)
        here = layer.astype(F32)
        first = ((facts[2:3] == here) & (facts[4:5] == slots)).astype(F32)
        second = ((facts[3:4] == here) & (facts[5:6] == slots)).astype(F32)
        chosen = (first + second).astype(BF16)
        step = 1024
        picked = boxes[kind][0]
        for begin in range(0, width, step):
            got = jnp.dot(chosen, view[:, begin:begin + step], preferred_element_type=F32)
            picked[source, :, :, begin:begin + step] = got.astype(BF16).reshape(plane, cap, step)
        if kind == 0:
            weights = jnp.sum(first * facts[0:1] + second * facts[1:2], axis=1, keepdims=True)
            tail = jnp.broadcast_to(weights, (batch, 128)).astype(BF16)
            picked[source, :, :, width:] = tail.reshape(plane, cap, 128)
        own_copy(source, kind).start()

        @pl.loop(1, plane)
        def _(off):
            spread(source, off, kind).start()

    def arrive(source, kind):
        own_copy(source, kind).wait()

        @pl.loop(1, plane)
        def _(off):
            spread(source, off, kind).wait_recv()

    def work(source):
        arrive(source, 0)
        row_x = rows_x[source, :, :, :width].reshape(batch, width)
        weight = rows_x[source, :, :, width:].reshape(batch, 128)[:, :1].astype(F32)
        both = jnp.dot(row_x, w_in[...], preferred_element_type=F32)
        arrive(source, 1)
        row_dy = rows_dy[source].reshape(batch, width)
        back_act = jnp.dot(row_dy, w_down[...], preferred_element_type=F32)
        gate_pre = both[:, :hidden]
        up_part = both[:, hidden:]
        sig = jax.nn.sigmoid(gate_pre)
        silu = gate_pre * sig
        act = silu * up_part
        gate_grad = jnp.sum(act * back_act, axis=1, keepdims=True)
        act_grad = weight * back_act
        gated[source] = (weight * act).astype(BF16)
        gate_side = act_grad * up_part * sig * (1.0 + gate_pre * (1.0 - sig))
        both_grads[source, :, :hidden] = gate_side.astype(BF16)
        both_grads[source, :, hidden:] = (act_grad * silu).astype(BF16)
        step = 512
        for begin in range(0, width, step):
            got = lax.dot_general(
                both_grads[source], w_in[begin:begin + step, :], (((1,), (1,)), ((), ())),
                preferred_element_type=F32)
            row_grads[source, :, :, begin:begin + step] = got.astype(BF16).reshape(
                plane, cap, step)
        row_grads[source, :, :, width:] = jnp.broadcast_to(gate_grad, (batch, 128)).astype(
            BF16).reshape(plane, cap, 128)

        @pl.loop(0, plane)
        def _(seat):
            mine = stays(source, seat)

            @pl.when(mine)
            def _():
                row_stay(seat // inner).start()

            @pl.when(jnp.logical_not(mine))
            def _():
                row_copy(source, seat).start()

    for part in range(PIECES):
        @pl.when(layer < outer - 1)
        def _():
            hop(layer, part, True, True).start()

        @pl.when(layer > 0)
        def _():
            hop(layer, part, False, True).start()
    pick(layer, x_ref, 0)
    pick(layer, dy_ref, 1)

    @pl.loop(1, outer + 1)
    def _(far):
        below = layer - far
        above = layer + far

        @pl.when(far < outer)
        def _():
            for kind, parts, box in ((0, (0, 1, 2), held_x), (1, (3, 4), held_dy)):
                for part in parts:
                    @pl.when(below >= 0)
                    def _():
                        hop(below, part, True, False).wait_recv()

                        @pl.when(layer < outer - 1)
                        def _():
                            hop(below, part, True, False).start()

                    @pl.when(above < outer)
                    def _():
                        hop(above, part, False, False).wait_recv()

                        @pl.when(layer > 0)
                        def _():
                            hop(above, part, False, False).start()

                @pl.loop(0, 2)
                def _(way):
                    source = layer + (2 * way - 1) * far

                    @pl.when((source >= 0) & (source < outer))
                    def _():
                        pick(source, box.at[source], kind)

        @pl.when(far == 1)
        def _():
            load_in.wait()
            load_down.wait()
            for swap in swaps:
                swap.wait()

            @pl.loop(0, width // 64)
            def _(i):
                at = pl.ds(pl.multiple_of(i * 64, 64), 64)
                own = flags[0:1, :1].astype(BF16)
                theirs = flags[1:2, :1].astype(BF16)
                w_in[at] = own * w_in[at] + theirs * other_in[at]
                w_down[at] = own * w_down[at] + theirs * other_down[at]

        @pl.loop(0, 2)
        def _(way):
            source = layer + (2 * way - 1) * (far - 1)

            @pl.when((source >= 0) & (source < outer) & (far + way > 1))
            def _():
                work(source)

    total = outer * batch
    grads = both_grads[...].reshape(total, 2 * hidden)
    acts = gated[...].reshape(total, hidden)

    def part_of(group, box, other):
        columns = pl.ds(pl.multiple_of(group * share, share), share)
        some = box[:, :, :, columns].reshape(total, share)
        return lax.dot_general(some, other, (((0,), (0,)), ((), ())), preferred_element_type=F32)

    kinds = (
        (rows_x, grads, sib_in, from_in, cross_in, got_in, grad_in_ref),
        (rows_dy, acts, sib_down, from_down, cross_down, got_down, grad_down_ref),
    )

    def to_sibling(kind, which):
        return remote(kinds[kind][2].at[which], kinds[kind][3].at[which],
                      sib_send.at[kind, which], sib_recv.at[kind, which], sibling)

    def to_across(kind):
        return remote(kinds[kind][4], kinds[kind][5], cross_send.at[kind], cross_recv.at[kind],
                      across)

    for which, target in ((0, 1 - side), (1, side)):
        for kind in range(2):
            box, other, sib = kinds[kind][:3]
            sib[which] = part_of(target * 2 + 1 - core, box, other).astype(BF16)
            to_sibling(kind, which).start()
        for kind in range(2):
            box, other, _, arrived, crossing, _, out = kinds[kind]
            mine = part_of(target * 2 + core, box, other)
            to_sibling(kind, which).wait_recv()
            joined = (mine + arrived[which].astype(F32)).astype(BF16)
            if which == 0:
                crossing[...] = joined
                to_across(kind).start()
            else:
                out[0] = joined
        if which == 0:
            swap_marks.wait()
            combine(1 - side, far_marks, far_sums)
            swap_sums.start()

    combine(side, marks, near_sums)
    swap_sums.wait()
    for begin in range(0, width, 512):
        at = slice(begin, begin + 512)
        tokens_ref[:, at] = (near_sums[:, at].astype(F32) + got_sums[:, at].astype(F32)).astype(BF16)
    gates_ref[...] = (
        near_sums[:, width:].astype(F32) + got_sums[:, width:].astype(F32)).astype(BF16)

    for kind in range(2):
        to_across(kind).wait()
        to_sibling(kind, 0).wait_send()
        to_sibling(kind, 1).wait_send()

    @pl.loop(0, share // 16)
    def _(i):
        at = pl.ds(pl.multiple_of(i * 16, 16), 16)
        for kind in range(2):
            got, out = kinds[kind][5:]
            near = out[0, at].astype(F32)
            away = got[at].astype(F32)
            lower = flags[2:3, :1]
            upper = flags[3:4, :1]
            out[0, at] = (lower * near + upper * away).astype(BF16)
            out[1, at] = (upper * near + lower * away).astype(BF16)

    for source in range(outer):
        @pl.loop(1, plane)
        def _(off):
            spread(source, off, 0).wait_send()
            spread(source, off, 1).wait_send()

        @pl.loop(0, plane)
        def _(seat):
            @pl.when(jnp.logical_not(stays(source, seat)))
            def _():
                row_copy(source, seat).wait_send()

        for part in range(PIECES):
            @pl.when((source <= layer) & (layer < outer - 1))
            def _():
                hop(source, part, True, False).wait_send()

            @pl.when((source >= layer) & (layer > 0))
            def _():
                hop(source, part, False, False).wait_send()


def expert_backward(rows_x, rows_dy, rows_gate, w_in, w_down):
    hidden = w_down.shape[1]
    both = jnp.dot(rows_x, w_in, preferred_element_type=jnp.float32)
    gate_pre = both[:, :hidden]
    up_part = both[:, hidden:]
    sigmoid_gate = jax.nn.sigmoid(gate_pre)
    silu_gate = gate_pre * sigmoid_gate
    activation = (silu_gate * up_part).astype(jnp.bfloat16)
    out_rows = lax.dot_general(
        activation, w_down, (((1,), (1,)), ((), ())), preferred_element_type=jnp.float32
    )
    gate_grad = jnp.sum(rows_dy.astype(jnp.float32) * out_rows, axis=1).astype(jnp.bfloat16)
    out_grad = (rows_gate.astype(jnp.float32)[:, None] * rows_dy.astype(jnp.float32)).astype(
        jnp.bfloat16
    )
    act_grad = jnp.dot(out_grad, w_down, preferred_element_type=jnp.float32)
    gate_grad_pre = act_grad * up_part * sigmoid_gate * (1.0 + gate_pre * (1.0 - sigmoid_gate))
    up_grad = act_grad * silu_gate
    both_grad = jnp.concatenate([gate_grad_pre, up_grad], axis=1).astype(jnp.bfloat16)
    row_grad = lax.dot_general(
        both_grad, w_in, (((1,), (1,)), ((), ())), preferred_element_type=jnp.float32
    ).astype(jnp.bfloat16)
    part_in = lax.dot_general(
        rows_x, both_grad, (((0,), (0,)), ((), ())), preferred_element_type=jnp.float32
    )
    part_down = lax.dot_general(
        out_grad, activation, (((0,), (0,)), ((), ())), preferred_element_type=jnp.float32
    )
    return (row_grad, gate_grad, part_in, part_down)


def plain_shards(tokens_in, grad_out, replica_of, gate_weights, placement, w_in_rep, w_down_rep):
    tok_count, model_width = tokens_in.shape
    top_count = replica_of.shape[1]
    group_count = lax.axis_size("grp")
    lane_count = lax.axis_size("ep")
    device_count = group_count * lane_count
    capacity = max(2, 2 * tok_count * top_count // device_count)
    w_in = w_in_rep[0, 0]
    w_down = w_down_rep[0, 0]
    dest_rows = replica_of.reshape(-1)
    row_count = tok_count * top_count
    row_ids = jnp.arange(row_count, dtype=jnp.int32)
    earlier = (dest_rows[:, None] == dest_rows[None, :]) & (row_ids[None, :] < row_ids[:, None])
    rank_in = jnp.sum(earlier.astype(jnp.int32), axis=1)
    send_slot = dest_rows * capacity + rank_in
    slot_table = jnp.full((device_count * capacity,), -1, jnp.int32).at[send_slot].set(row_ids)
    is_live = slot_table >= 0
    safe_ids = jnp.maximum(slot_table, 0)
    token_ids = safe_ids // top_count
    send_x = jnp.where(is_live[:, None], tokens_in[token_ids], jnp.zeros((), tokens_in.dtype))
    send_dy = jnp.where(is_live[:, None], grad_out[token_ids], jnp.zeros((), grad_out.dtype))
    send_gate = jnp.where(
        is_live, gate_weights.reshape(-1)[safe_ids], jnp.zeros((), gate_weights.dtype)
    )
    block_shape = (group_count, lane_count, capacity, model_width)
    outgoing = (
        send_x.reshape(block_shape),
        send_dy.reshape(block_shape),
        send_gate.reshape(group_count, lane_count, capacity),
    )
    arrived = (
        lax.all_to_all(
            lax.all_to_all(outgoing[0], "ep", split_axis=1, concat_axis=1, tiled=True),
            "grp",
            split_axis=0,
            concat_axis=0,
            tiled=True,
        ),
        lax.all_to_all(
            lax.all_to_all(outgoing[1], "ep", split_axis=1, concat_axis=1, tiled=True),
            "grp",
            split_axis=0,
            concat_axis=0,
            tiled=True,
        ),
        lax.all_to_all(
            lax.all_to_all(outgoing[2], "ep", split_axis=1, concat_axis=1, tiled=True),
            "grp",
            split_axis=0,
            concat_axis=0,
            tiled=True,
        ),
    )
    rows_x = arrived[0].reshape(device_count * capacity, model_width)
    rows_dy = arrived[1].reshape(device_count * capacity, model_width)
    rows_gate = arrived[2].reshape(device_count * capacity)
    row_grad, gate_grad, part_in, part_down = expert_backward(
        rows_x, rows_dy, rows_gate, w_in, w_down
    )
    returning = (
        row_grad.reshape(block_shape),
        gate_grad.reshape(group_count, lane_count, capacity),
    )
    came_back = (
        lax.all_to_all(
            lax.all_to_all(returning[0], "grp", split_axis=0, concat_axis=0, tiled=True),
            "ep",
            split_axis=1,
            concat_axis=1,
            tiled=True,
        ),
        lax.all_to_all(
            lax.all_to_all(returning[1], "grp", split_axis=0, concat_axis=0, tiled=True),
            "ep",
            split_axis=1,
            concat_axis=1,
            tiled=True,
        ),
    )
    grads_rows = came_back[0].reshape(device_count * capacity, model_width)[send_slot]
    d_tokens = jnp.sum(
        grads_rows.reshape(tok_count, top_count, model_width).astype(jnp.float32), axis=1
    ).astype(jnp.bfloat16)
    d_gates = came_back[1].reshape(-1)[send_slot].reshape(tok_count, top_count)
    group_index = lax.axis_index("grp")
    column_index = lax.axis_index("ep")
    my_slot = placement[group_index, column_index]
    slot_mask = (jnp.arange(KPC, dtype=jnp.int32) == my_slot).astype(jnp.float32)
    stack_in = slot_mask[:, None, None] * part_in[None]
    stack_down = slot_mask[:, None, None] * part_down[None]
    summed_in, summed_down = (
        lax.psum_scatter(
            stack_in.astype(jnp.bfloat16), "grp", scatter_dimension=1, tiled=True
        ).astype(jnp.float32),
        lax.psum_scatter(
            stack_down.astype(jnp.bfloat16), "grp", scatter_dimension=1, tiled=True
        ).astype(jnp.float32),
    )
    return (d_tokens, d_gates, summed_in.astype(jnp.bfloat16), summed_down.astype(jnp.bfloat16))


def shards(tokens_in, grad_out, replica_of, gate_weights, placement, w_in_rep, w_down_rep):
    tok_count, width = tokens_in.shape
    top_count = replica_of.shape[1]
    groups = lax.axis_size("grp")
    lanes = lax.axis_size("ep")
    devices = groups * lanes
    cap = max(2, 2 * tok_count * top_count // devices)
    if cap % 16 or top_count != 2 or groups != 4:
        return plain_shards(
            tokens_in, grad_out, replica_of, gate_weights, placement, w_in_rep, w_down_rep
        )
    inner = max(1, min(lanes, tok_count // (groups * cap)))
    outer = lanes // inner
    plane = groups // 2 * inner
    senders = groups // 2 * lanes
    w_in = w_in_rep[0, 0]
    w_down = w_down_rep[0, 0]
    hidden = w_down.shape[1]
    routes = jnp.concatenate(
        [
            replica_of.astype(F32),
            gate_weights.astype(F32),
            jnp.zeros((tok_count, 128 - 2 * top_count), F32),
        ],
        axis=1,
    )
    copies = jnp.pad(
        jnp.tile(placement, (1, groups)).astype(F32), ((0, 8 - groups), (0, 128 - devices))
    )
    rows_each = cap
    cap = (groups - 1) * cap
    full = width + 128
    any_spec = pl.BlockSpec(memory_space=pl.ANY)
    vmem_spec = pl.BlockSpec(memory_space=pltpu.VMEM)
    dma = pltpu.SemaphoreType.DMA
    share = width // groups
    batch = plane * cap
    d_tokens, gates, grad_in, grad_down = pl.pallas_call(
        functools.partial(layer_kernel, groups, lanes, inner, rows_each),
        out_shape=(
            jax.ShapeDtypeStruct((tok_count, width), BF16),
            jax.ShapeDtypeStruct((tok_count, 128), BF16),
            jax.ShapeDtypeStruct((KPC, share, 2 * hidden), BF16),
            jax.ShapeDtypeStruct((KPC, share, hidden), BF16),
        ),
        in_specs=[vmem_spec] * 4 + [any_spec] * 2,
        out_specs=(vmem_spec,) * 4,
        scratch_shapes=[
            pltpu.VMEM((outer, tok_count, 128), BF16),
            pltpu.VMEM((outer, tok_count, width), BF16),
            pltpu.VMEM((outer, tok_count, width), BF16),
            pltpu.VMEM((outer, plane, cap, full), BF16),
            pltpu.VMEM((outer, plane, cap, width), BF16),
            pltpu.VMEM((outer, plane, cap, full), BF16),
            pltpu.VMEM((outer, plane, cap, width), BF16),
            pltpu.VMEM((tok_count, 128), F32),
            pltpu.VMEM((tok_count, 128), F32),
            pltpu.VMEM((8, 128), F32),
            pltpu.VMEM((tok_count, full), BF16),
            pltpu.VMEM((tok_count, full), BF16),
            pltpu.VMEM((tok_count, full), BF16),
            pltpu.VMEM((width, 2 * hidden), BF16),
            pltpu.VMEM((width, hidden), BF16),
            pltpu.VMEM((width, 2 * hidden), BF16),
            pltpu.VMEM((width, hidden), BF16),
            pltpu.VMEM((outer, batch, 2 * hidden), BF16),
            pltpu.VMEM((outer, batch, hidden), BF16),
            pltpu.VMEM((outer, plane, cap, width + 128), BF16),
            pltpu.VMEM((senders, cap, width + 128), BF16),
            pltpu.VMEM((2, share, 2 * hidden), BF16),
            pltpu.VMEM((2, share, hidden), BF16),
            pltpu.VMEM((2, share, 2 * hidden), BF16),
            pltpu.VMEM((2, share, hidden), BF16),
            pltpu.VMEM((share, 2 * hidden), BF16),
            pltpu.VMEM((share, hidden), BF16),
            pltpu.VMEM((share, 2 * hidden), BF16),
            pltpu.VMEM((share, hidden), BF16),
            dma((outer, PIECES)),
            dma((outer, PIECES)),
            dma((outer, PIECES)),
            dma((2, outer, plane)),
            dma((2, outer, plane)),
            dma((2, outer)),
            dma((2,)),
            dma((outer, plane)),
            dma((senders,)),
            dma((2,)),
            dma((2,)),
            dma((2,)),
            dma((2, 2)),
            dma((2, 2)),
            dma((2,)),
            dma((2,)),
            dma((2,)),
            dma((2,)),
        ],
        compiler_params=pltpu.CompilerParams(
            collective_id=0, has_side_effects=True, vmem_limit_bytes=58 * 2**20
        ),
        name="layer_backward",
    )(tokens_in, grad_out, routes, copies, w_in, w_down)
    return d_tokens, gates[:, :top_count], grad_in, grad_down


def solution(mesh):
    placed = (
        P(("grp", "ep"), None),
        P(("grp", "ep"), None),
        P(("grp", "ep"), None),
        P(("grp", "ep"), None),
        P(),
        P("grp", "ep", None, None),
        P("grp", "ep", None, None),
    )
    return jax.shard_map(
        shards,
        mesh=mesh,
        in_specs=placed,
        out_specs=(
            P(("grp", "ep"), None),
            P(("grp", "ep"), None),
            P("ep", "grp", None),
            P("ep", "grp", None),
        ),
        check_vma=False,
    )
```

```python
import functools

import jax
import jax.numpy as jnp
from jax import lax
from jax.experimental import pallas as pl
from jax.experimental.pallas import tpu as pltpu
from jax.sharding import PartitionSpec as P

KPC = 2
MESH = pl.DeviceIdType.MESH
F32 = jnp.float32
BF16 = jnp.bfloat16
PIECES = 5


def layer_kernel(groups, lanes, inner, cap, x_ref, dy_ref, routes_ref, copies_ref,
                 w_in_hbm, w_down_hbm,
                 tokens_ref, gates_ref, grad_in_ref, grad_down_ref,
                 held_facts, held_x, held_dy, picked_x, picked_dy, rows_x, rows_dy, marks, flags,
                 w_in, w_down, other_in, other_down,
                 both_grads, gated, row_grads, back,
                 sib_in, sib_down, from_in, from_down, cross_in, cross_down, got_in, got_down,
                 up_send, down_send, chain_recv, plane_send, plane_recv, own_sem, load_sem,
                 row_send, row_recv, row_own, swap_send, swap_recv, sib_send, sib_recv,
                 cross_send, cross_recv):
    tok_count, width = x_ref.shape
    full = width + 128
    rows_each = cap
    cap = (groups - 1) * cap
    hidden = w_down.shape[1]
    outer = lanes // inner
    plane = groups // 2 * inner
    devices = groups * lanes
    batch = plane * cap
    senders = groups // 2 * lanes
    share = width // groups
    my_group = lax.axis_index("grp")
    my_lane = lax.axis_index("ep")
    me = my_group * lanes + my_lane
    layer = my_lane // inner
    side = my_group // 2
    core = lax.rem(my_group, 2)
    my_seat = side * inner + lax.rem(my_lane, inner)
    my_sender = side * lanes + my_lane
    sibling = (side * 2 + 1 - core, my_lane)
    across = ((1 - side) * 2 + core, my_lane)
    half = tok_count // 2

    load_in = pltpu.make_async_copy(w_in_hbm, w_in, load_sem.at[0])
    load_down = pltpu.make_async_copy(w_down_hbm, w_down, load_sem.at[1])
    load_in.start()
    load_down.start()

    barrier = pltpu.get_barrier_semaphore()

    @pl.loop(1, devices)
    def _(off):
        peer = lax.rem(me + off, devices)
        pl.semaphore_signal(barrier, inc=1, device_id=(peer // lanes, lax.rem(peer, lanes)),
                            device_id_type=MESH)

    device_ids = lax.broadcasted_iota(jnp.int32, (1, 128), 1)
    group_ids = device_ids // lanes
    lane_in = device_ids - group_ids * lanes
    copies = [copies_ref[group:group + 1] for group in range(groups)]
    low = jnp.where((copies[2] != copies[0]) | (copies[3] != copies[0]), copies[0], copies[1])
    mine = sum(jnp.where(group_ids == group, copies[group], 0.0) for group in range(groups))
    side_table = (mine != low).astype(F32)
    copy_table = sum(
        ((copies[group] == mine) & (group_ids > group)).astype(F32) for group in range(groups))
    layer_table = (lane_in // inner).astype(F32)
    within_table = lax.rem(lane_in, inner).astype(F32)
    copy_base = copy_table * rows_each
    place_table = (side_table * inner + within_table) * cap + copy_base
    back_table = (side_table * lanes + lane_in.astype(F32)) * cap + copy_base
    here_only = device_ids == me
    my_low = jnp.sum(jnp.where(here_only, low, 0.0), axis=1, keepdims=True)
    my_held = jnp.sum(jnp.where(here_only, mine, 0.0), axis=1, keepdims=True)
    on_high = side.astype(F32)
    my_expert = my_low * (1.0 - on_high) + (1.0 - my_low) * on_high
    flags[0:1] = jnp.broadcast_to((my_held == my_expert).astype(F32), (1, 128))
    flags[1:2] = jnp.broadcast_to((my_held != my_expert).astype(F32), (1, 128))
    flags[2:3] = jnp.broadcast_to(1.0 - my_expert, (1, 128))
    flags[3:4] = jnp.broadcast_to(my_expert, (1, 128))
    routes = routes_ref[...]
    across_tokens = routes.T
    token_ids = lax.broadcasted_iota(jnp.int32, (tok_count, tok_count), 0)
    other_ids = lax.broadcasted_iota(jnp.int32, (tok_count, tok_count), 1)
    earlier = other_ids < token_ids
    column_ids = lax.broadcasted_iota(jnp.int32, (tok_count, 128), 1)
    spread_ids = column_ids.astype(F32)
    facts = jnp.where(column_ids < 2, pltpu.roll(routes, 126, 1), 0.0)
    backs = jnp.zeros((tok_count, 128), F32)
    for k in range(2):
        named = routes[:, k:k + 1]
        same = (named == across_tokens[0:1]).astype(F32) + (named == across_tokens[1:2]).astype(F32)
        rank = jnp.sum(jnp.where(earlier, same, 0.0), axis=1, keepdims=True)
        chosen = named == spread_ids

        def look(table):
            return jnp.sum(jnp.where(chosen, table, 0.0), axis=1, keepdims=True)

        facts = jnp.where(column_ids == 2 + k, look(layer_table), facts)
        facts = jnp.where(column_ids == 4 + k, look(place_table) + rank, facts)
        backs = jnp.where(column_ids == k, look(back_table) + rank, backs)
    held_facts[layer] = facts.astype(BF16)
    marks[...] = backs

    pl.semaphore_wait(barrier, devices - 1)

    def remote(src, dst, send, recv, device):
        return pltpu.make_async_remote_copy(
            src_ref=src, dst_ref=dst, send_sem=send, recv_sem=recv,
            device_id=device, device_id_type=MESH)

    swaps = [
        remote(w_in_hbm, other_in, swap_send.at[0], swap_recv.at[0], sibling),
        remote(w_down_hbm, other_down, swap_send.at[1], swap_recv.at[1], sibling),
    ]
    def hop(source, part, upward, own):
        if part == 0:
            src = dst = held_facts.at[source]
        else:
            box, given = (held_x, x_ref) if part < 3 else (held_dy, dy_ref)
            at = pl.ds((part - 1) % 2 * half, half)
            dst = box.at[source, at]
            src = given.at[at] if own else dst
        sems = up_send if upward else down_send
        return remote(src, dst, sems.at[source, part], chain_recv.at[source, part],
                      (my_group, my_lane + inner if upward else my_lane - inner))

    boxes = ((picked_x, rows_x), (picked_dy, rows_dy))

    def spread(source, off, kind):
        seat = lax.rem(my_seat + off, plane)
        src, dst = boxes[kind]
        return remote(src.at[source, seat], dst.at[source, my_seat],
                      plane_send.at[kind, source, off], plane_recv.at[kind, source, off],
                      (seat // inner * 2 + core, layer * inner + lax.rem(seat, inner)))

    def own_copy(source, kind):
        src, dst = boxes[kind]
        return pltpu.make_async_copy(
            src.at[source, my_seat], dst.at[source, my_seat], own_sem.at[kind, source])

    def row_copy(source, seat):
        return pltpu.make_async_remote_copy(
            src_ref=row_grads.at[source, seat],
            dst_ref=back.at[my_sender],
            send_sem=row_send.at[source, seat],
            recv_sem=row_recv.at[my_sender],
            device_id=(seat // inner * 2 + core, source * inner + lax.rem(seat, inner)),
            device_id_type=MESH,
        )

    def row_arrival(peer):
        return pltpu.make_async_remote_copy(
            src_ref=row_grads.at[0, 0],
            dst_ref=back.at[peer],
            send_sem=row_send.at[0, 0],
            recv_sem=row_recv.at[peer],
            device_id=(peer // lanes * 2 + core, lax.rem(peer, lanes)),
            device_id_type=MESH,
        )

    row_stay = pltpu.make_async_copy(row_grads.at[layer, my_seat], back.at[my_sender], row_own)

    def pick(source, view, kind):
        facts = held_facts[source].astype(F32).T
        slots = lax.broadcasted_iota(jnp.int32, (batch, tok_count), 0).astype(F32)
        here = layer.astype(F32)
        first = ((facts[2:3] == here) & (facts[4:5] == slots)).astype(F32)
        second = ((facts[3:4] == here) & (facts[5:6] == slots)).astype(F32)
        chosen = (first + second).astype(BF16)
        step = 1024
        picked = boxes[kind][0]
        for begin in range(0, width, step):
            got = jnp.dot(chosen, view[:, begin:begin + step], preferred_element_type=F32)
            picked[source, :, :, begin:begin + step] = got.astype(BF16).reshape(plane, cap, step)
        if kind == 0:
            weights = jnp.sum(first * facts[0:1] + second * facts[1:2], axis=1, keepdims=True)
            tail = jnp.broadcast_to(weights, (batch, 128)).astype(BF16)
            picked[source, :, :, width:] = tail.reshape(plane, cap, 128)
        own_copy(source, kind).start()

        @pl.loop(1, plane)
        def _(off):
            spread(source, off, kind).start()

    def arrive(source, kind):
        own_copy(source, kind).wait()

        @pl.loop(1, plane)
        def _(off):
            spread(source, off, kind).wait_recv()

    def work(source):
        arrive(source, 0)
        row_x = rows_x[source, :, :, :width].reshape(batch, width)
        weight = rows_x[source, :, :, width:].reshape(batch, 128)[:, :1].astype(F32)
        both = jnp.dot(row_x, w_in[...], preferred_element_type=F32)
        arrive(source, 1)
        row_dy = rows_dy[source].reshape(batch, width)
        back_act = jnp.dot(row_dy, w_down[...], preferred_element_type=F32)
        gate_pre = both[:, :hidden]
        up_part = both[:, hidden:]
        sig = jax.nn.sigmoid(gate_pre)
        silu = gate_pre * sig
        act = silu * up_part
        gate_grad = jnp.sum(act * back_act, axis=1, keepdims=True)
        act_grad = weight * back_act
        gated[source] = (weight * act).astype(BF16)
        gate_side = act_grad * up_part * sig * (1.0 + gate_pre * (1.0 - sig))
        both_grads[source, :, :hidden] = gate_side.astype(BF16)
        both_grads[source, :, hidden:] = (act_grad * silu).astype(BF16)
        step = 512
        for begin in range(0, width, step):
            got = lax.dot_general(
                both_grads[source], w_in[begin:begin + step, :], (((1,), (1,)), ((), ())),
                preferred_element_type=F32)
            row_grads[source, :, :, begin:begin + step] = got.astype(BF16).reshape(
                plane, cap, step)
        row_grads[source, :, :, width:] = jnp.broadcast_to(gate_grad, (batch, 128)).astype(
            BF16).reshape(plane, cap, 128)

        @pl.loop(0, plane)
        def _(seat):
            mine = (source == layer) & (seat == my_seat)

            @pl.when(mine)
            def _():
                row_stay.start()

            @pl.when(jnp.logical_not(mine))
            def _():
                row_copy(source, seat).start()

    for part in range(PIECES):
        @pl.when(layer < outer - 1)
        def _():
            hop(layer, part, True, True).start()

        @pl.when(layer > 0)
        def _():
            hop(layer, part, False, True).start()
    pick(layer, x_ref, 0)
    pick(layer, dy_ref, 1)
    for swap in swaps:
        swap.start()

    @pl.loop(1, outer + 1)
    def _(far):
        below = layer - far
        above = layer + far

        @pl.when(far < outer)
        def _():
            for kind, parts, box in ((0, (0, 1, 2), held_x), (1, (3, 4), held_dy)):
                for part in parts:
                    @pl.when(below >= 0)
                    def _():
                        hop(below, part, True, False).wait_recv()

                        @pl.when(layer < outer - 1)
                        def _():
                            hop(below, part, True, False).start()

                    @pl.when(above < outer)
                    def _():
                        hop(above, part, False, False).wait_recv()

                        @pl.when(layer > 0)
                        def _():
                            hop(above, part, False, False).start()

                @pl.loop(0, 2)
                def _(way):
                    source = layer + (2 * way - 1) * far

                    @pl.when((source >= 0) & (source < outer))
                    def _():
                        pick(source, box.at[source], kind)

        @pl.when(far == 1)
        def _():
            load_in.wait()
            load_down.wait()
            for swap in swaps:
                swap.wait()

            @pl.loop(0, width // 64)
            def _(i):
                at = pl.ds(pl.multiple_of(i * 64, 64), 64)
                own = flags[0:1, :1].astype(BF16)
                theirs = flags[1:2, :1].astype(BF16)
                w_in[at] = own * w_in[at] + theirs * other_in[at]
                w_down[at] = own * w_down[at] + theirs * other_down[at]

        @pl.loop(0, 2)
        def _(way):
            source = layer + (2 * way - 1) * (far - 1)

            @pl.when((source >= 0) & (source < outer) & (far + way > 1))
            def _():
                work(source)

    total = outer * batch
    grads = both_grads[...].reshape(total, 2 * hidden)
    acts = gated[...].reshape(total, hidden)

    def part_of(group, box, other):
        columns = pl.ds(pl.multiple_of(group * share, share), share)
        some = box[:, :, :, columns].reshape(total, share)
        return lax.dot_general(some, other, (((0,), (0,)), ((), ())), preferred_element_type=F32)

    kinds = (
        (rows_x, grads, sib_in, from_in, cross_in, got_in, grad_in_ref),
        (rows_dy, acts, sib_down, from_down, cross_down, got_down, grad_down_ref),
    )

    def to_sibling(kind, which):
        return remote(kinds[kind][2].at[which], kinds[kind][3].at[which],
                      sib_send.at[kind, which], sib_recv.at[kind, which], sibling)

    def to_across(kind):
        return remote(kinds[kind][4], kinds[kind][5], cross_send.at[kind], cross_recv.at[kind],
                      across)

    for which, target in ((0, 1 - side), (1, side)):
        for kind in range(2):
            box, other, sib = kinds[kind][:3]
            sib[which] = part_of(target * 2 + 1 - core, box, other).astype(BF16)
            to_sibling(kind, which).start()
        for kind in range(2):
            box, other, _, arrived, crossing, _, out = kinds[kind]
            mine = part_of(target * 2 + core, box, other)
            to_sibling(kind, which).wait_recv()
            joined = (mine + arrived[which].astype(F32)).astype(BF16)
            if which == 0:
                crossing[...] = joined
                to_across(kind).start()
            else:
                out[0] = joined

    row_stay.wait()

    @pl.loop(1, senders)
    def _(off):
        row_arrival(lax.rem(my_sender + off, senders)).wait_recv()

    places = lax.broadcasted_iota(jnp.int32, (tok_count, senders * cap), 1).astype(F32)
    first = (marks[:, 0:1] == places).astype(F32)
    second = (marks[:, 1:2] == places).astype(F32)
    chosen = (first + second).astype(BF16)
    for begin in range(0, width, 512):
        view = back[:, :, begin:begin + 512].reshape(senders * cap, 512)
        tokens_ref[:, begin:begin + 512] = jnp.dot(
            chosen, view, preferred_element_type=F32).astype(BF16)
    tail = back[:, :, width:].reshape(senders * cap, 128)
    gate_first = jnp.dot(first.astype(BF16), tail, preferred_element_type=F32)
    gate_second = jnp.dot(second.astype(BF16), tail, preferred_element_type=F32)
    lane_ids = lax.broadcasted_iota(jnp.int32, (tok_count, 128), 1)
    gates_ref[...] = jnp.where(lane_ids == 0, gate_first, gate_second).astype(BF16)

    for kind in range(2):
        to_across(kind).wait()
        to_sibling(kind, 0).wait_send()
        to_sibling(kind, 1).wait_send()

    @pl.loop(0, share // 16)
    def _(i):
        at = pl.ds(pl.multiple_of(i * 16, 16), 16)
        for kind in range(2):
            got, out = kinds[kind][5:]
            near = out[0, at].astype(F32)
            away = got[at].astype(F32)
            lower = flags[2:3, :1]
            upper = flags[3:4, :1]
            out[0, at] = (lower * near + upper * away).astype(BF16)
            out[1, at] = (upper * near + lower * away).astype(BF16)

    for source in range(outer):
        @pl.loop(1, plane)
        def _(off):
            spread(source, off, 0).wait_send()
            spread(source, off, 1).wait_send()

        @pl.loop(0, plane)
        def _(seat):
            @pl.when(jnp.logical_not((source == layer) & (seat == my_seat)))
            def _():
                row_copy(source, seat).wait_send()

        for part in range(PIECES):
            @pl.when((source <= layer) & (layer < outer - 1))
            def _():
                hop(source, part, True, False).wait_send()

            @pl.when((source >= layer) & (layer > 0))
            def _():
                hop(source, part, False, False).wait_send()


def expert_backward(rows_x, rows_dy, rows_gate, w_in, w_down):
    hidden = w_down.shape[1]
    both = jnp.dot(rows_x, w_in, preferred_element_type=jnp.float32)
    gate_pre = both[:, :hidden]
    up_part = both[:, hidden:]
    sigmoid_gate = jax.nn.sigmoid(gate_pre)
    silu_gate = gate_pre * sigmoid_gate
    activation = (silu_gate * up_part).astype(jnp.bfloat16)
    out_rows = lax.dot_general(
        activation, w_down, (((1,), (1,)), ((), ())), preferred_element_type=jnp.float32
    )
    gate_grad = jnp.sum(rows_dy.astype(jnp.float32) * out_rows, axis=1).astype(jnp.bfloat16)
    out_grad = (rows_gate.astype(jnp.float32)[:, None] * rows_dy.astype(jnp.float32)).astype(
        jnp.bfloat16
    )
    act_grad = jnp.dot(out_grad, w_down, preferred_element_type=jnp.float32)
    gate_grad_pre = act_grad * up_part * sigmoid_gate * (1.0 + gate_pre * (1.0 - sigmoid_gate))
    up_grad = act_grad * silu_gate
    both_grad = jnp.concatenate([gate_grad_pre, up_grad], axis=1).astype(jnp.bfloat16)
    row_grad = lax.dot_general(
        both_grad, w_in, (((1,), (1,)), ((), ())), preferred_element_type=jnp.float32
    ).astype(jnp.bfloat16)
    part_in = lax.dot_general(
        rows_x, both_grad, (((0,), (0,)), ((), ())), preferred_element_type=jnp.float32
    )
    part_down = lax.dot_general(
        out_grad, activation, (((0,), (0,)), ((), ())), preferred_element_type=jnp.float32
    )
    return (row_grad, gate_grad, part_in, part_down)


def plain_shards(tokens_in, grad_out, replica_of, gate_weights, placement, w_in_rep, w_down_rep):
    tok_count, model_width = tokens_in.shape
    top_count = replica_of.shape[1]
    group_count = lax.axis_size("grp")
    lane_count = lax.axis_size("ep")
    device_count = group_count * lane_count
    capacity = max(2, 2 * tok_count * top_count // device_count)
    w_in = w_in_rep[0, 0]
    w_down = w_down_rep[0, 0]
    dest_rows = replica_of.reshape(-1)
    row_count = tok_count * top_count
    row_ids = jnp.arange(row_count, dtype=jnp.int32)
    earlier = (dest_rows[:, None] == dest_rows[None, :]) & (row_ids[None, :] < row_ids[:, None])
    rank_in = jnp.sum(earlier.astype(jnp.int32), axis=1)
    send_slot = dest_rows * capacity + rank_in
    slot_table = jnp.full((device_count * capacity,), -1, jnp.int32).at[send_slot].set(row_ids)
    is_live = slot_table >= 0
    safe_ids = jnp.maximum(slot_table, 0)
    token_ids = safe_ids // top_count
    send_x = jnp.where(is_live[:, None], tokens_in[token_ids], jnp.zeros((), tokens_in.dtype))
    send_dy = jnp.where(is_live[:, None], grad_out[token_ids], jnp.zeros((), grad_out.dtype))
    send_gate = jnp.where(
        is_live, gate_weights.reshape(-1)[safe_ids], jnp.zeros((), gate_weights.dtype)
    )
    block_shape = (group_count, lane_count, capacity, model_width)
    outgoing = (
        send_x.reshape(block_shape),
        send_dy.reshape(block_shape),
        send_gate.reshape(group_count, lane_count, capacity),
    )
    arrived = (
        lax.all_to_all(
            lax.all_to_all(outgoing[0], "ep", split_axis=1, concat_axis=1, tiled=True),
            "grp",
            split_axis=0,
            concat_axis=0,
            tiled=True,
        ),
        lax.all_to_all(
            lax.all_to_all(outgoing[1], "ep", split_axis=1, concat_axis=1, tiled=True),
            "grp",
            split_axis=0,
            concat_axis=0,
            tiled=True,
        ),
        lax.all_to_all(
            lax.all_to_all(outgoing[2], "ep", split_axis=1, concat_axis=1, tiled=True),
            "grp",
            split_axis=0,
            concat_axis=0,
            tiled=True,
        ),
    )
    rows_x = arrived[0].reshape(device_count * capacity, model_width)
    rows_dy = arrived[1].reshape(device_count * capacity, model_width)
    rows_gate = arrived[2].reshape(device_count * capacity)
    row_grad, gate_grad, part_in, part_down = expert_backward(
        rows_x, rows_dy, rows_gate, w_in, w_down
    )
    returning = (
        row_grad.reshape(block_shape),
        gate_grad.reshape(group_count, lane_count, capacity),
    )
    came_back = (
        lax.all_to_all(
            lax.all_to_all(returning[0], "grp", split_axis=0, concat_axis=0, tiled=True),
            "ep",
            split_axis=1,
            concat_axis=1,
            tiled=True,
        ),
        lax.all_to_all(
            lax.all_to_all(returning[1], "grp", split_axis=0, concat_axis=0, tiled=True),
            "ep",
            split_axis=1,
            concat_axis=1,
            tiled=True,
        ),
    )
    grads_rows = came_back[0].reshape(device_count * capacity, model_width)[send_slot]
    d_tokens = jnp.sum(
        grads_rows.reshape(tok_count, top_count, model_width).astype(jnp.float32), axis=1
    ).astype(jnp.bfloat16)
    d_gates = came_back[1].reshape(-1)[send_slot].reshape(tok_count, top_count)
    group_index = lax.axis_index("grp")
    column_index = lax.axis_index("ep")
    my_slot = placement[group_index, column_index]
    slot_mask = (jnp.arange(KPC, dtype=jnp.int32) == my_slot).astype(jnp.float32)
    stack_in = slot_mask[:, None, None] * part_in[None]
    stack_down = slot_mask[:, None, None] * part_down[None]
    summed_in, summed_down = (
        lax.psum_scatter(
            stack_in.astype(jnp.bfloat16), "grp", scatter_dimension=1, tiled=True
        ).astype(jnp.float32),
        lax.psum_scatter(
            stack_down.astype(jnp.bfloat16), "grp", scatter_dimension=1, tiled=True
        ).astype(jnp.float32),
    )
    return (d_tokens, d_gates, summed_in.astype(jnp.bfloat16), summed_down.astype(jnp.bfloat16))


def shards(tokens_in, grad_out, replica_of, gate_weights, placement, w_in_rep, w_down_rep):
    tok_count, width = tokens_in.shape
    top_count = replica_of.shape[1]
    groups = lax.axis_size("grp")
    lanes = lax.axis_size("ep")
    devices = groups * lanes
    cap = max(2, 2 * tok_count * top_count // devices)
    if cap % 16 or top_count != 2 or groups != 4:
        return plain_shards(
            tokens_in, grad_out, replica_of, gate_weights, placement, w_in_rep, w_down_rep
        )
    inner = max(1, min(lanes, tok_count // (groups * cap)))
    outer = lanes // inner
    plane = groups // 2 * inner
    senders = groups // 2 * lanes
    w_in = w_in_rep[0, 0]
    w_down = w_down_rep[0, 0]
    hidden = w_down.shape[1]
    routes = jnp.concatenate(
        [
            replica_of.astype(F32),
            gate_weights.astype(F32),
            jnp.zeros((tok_count, 128 - 2 * top_count), F32),
        ],
        axis=1,
    )
    copies = jnp.pad(
        jnp.tile(placement, (1, groups)).astype(F32), ((0, 8 - groups), (0, 128 - devices))
    )
    rows_each = cap
    cap = (groups - 1) * cap
    full = width + 128
    any_spec = pl.BlockSpec(memory_space=pl.ANY)
    vmem_spec = pl.BlockSpec(memory_space=pltpu.VMEM)
    dma = pltpu.SemaphoreType.DMA
    share = width // groups
    batch = plane * cap
    d_tokens, gates, grad_in, grad_down = pl.pallas_call(
        functools.partial(layer_kernel, groups, lanes, inner, rows_each),
        out_shape=(
            jax.ShapeDtypeStruct((tok_count, width), BF16),
            jax.ShapeDtypeStruct((tok_count, 128), BF16),
            jax.ShapeDtypeStruct((KPC, share, 2 * hidden), BF16),
            jax.ShapeDtypeStruct((KPC, share, hidden), BF16),
        ),
        in_specs=[vmem_spec] * 4 + [any_spec] * 2,
        out_specs=(vmem_spec,) * 4,
        scratch_shapes=[
            pltpu.VMEM((outer, tok_count, 128), BF16),
            pltpu.VMEM((outer, tok_count, width), BF16),
            pltpu.VMEM((outer, tok_count, width), BF16),
            pltpu.VMEM((outer, plane, cap, full), BF16),
            pltpu.VMEM((outer, plane, cap, width), BF16),
            pltpu.VMEM((outer, plane, cap, full), BF16),
            pltpu.VMEM((outer, plane, cap, width), BF16),
            pltpu.VMEM((tok_count, 128), F32),
            pltpu.VMEM((8, 128), F32),
            pltpu.VMEM((width, 2 * hidden), BF16),
            pltpu.VMEM((width, hidden), BF16),
            pltpu.VMEM((width, 2 * hidden), BF16),
            pltpu.VMEM((width, hidden), BF16),
            pltpu.VMEM((outer, batch, 2 * hidden), BF16),
            pltpu.VMEM((outer, batch, hidden), BF16),
            pltpu.VMEM((outer, plane, cap, width + 128), BF16),
            pltpu.VMEM((senders, cap, width + 128), BF16),
            pltpu.VMEM((2, share, 2 * hidden), BF16),
            pltpu.VMEM((2, share, hidden), BF16),
            pltpu.VMEM((2, share, 2 * hidden), BF16),
            pltpu.VMEM((2, share, hidden), BF16),
            pltpu.VMEM((share, 2 * hidden), BF16),
            pltpu.VMEM((share, hidden), BF16),
            pltpu.VMEM((share, 2 * hidden), BF16),
            pltpu.VMEM((share, hidden), BF16),
            dma((outer, PIECES)),
            dma((outer, PIECES)),
            dma((outer, PIECES)),
            dma((2, outer, plane)),
            dma((2, outer, plane)),
            dma((2, outer)),
            dma((2,)),
            dma((outer, plane)),
            dma((senders,)),
            dma,
            dma((2,)),
            dma((2,)),
            dma((2, 2)),
            dma((2, 2)),
            dma((2,)),
            dma((2,)),
        ],
        compiler_params=pltpu.CompilerParams(
            collective_id=0, has_side_effects=True, vmem_limit_bytes=58 * 2**20
        ),
        name="layer_backward",
    )(tokens_in, grad_out, routes, copies, w_in, w_down)
    return d_tokens, gates[:, :top_count], grad_in, grad_down


def solution(mesh):
    placed = (
        P(("grp", "ep"), None),
        P(("grp", "ep"), None),
        P(("grp", "ep"), None),
        P(("grp", "ep"), None),
        P(),
        P("grp", "ep", None, None),
        P("grp", "ep", None, None),
    )
    return jax.shard_map(
        shards,
        mesh=mesh,
        in_specs=placed,
        out_specs=(
            P(("grp", "ep"), None),
            P(("grp", "ep"), None),
            P("ep", "grp", None),
            P("ep", "grp", None),
        ),
        check_vma=False,
    )
```
